256 devices in a mesh: group: 8 (over x, core), expert: 32 (over y, z).
Axes of the slice: x: 4, y: 4, z: 8, core: 2. Of those that a mesh axis runs over, the one named last changes fastest.
Arguments:
- resid: bfloat16 [32768, 2048], P(('group', 'expert')), may hold values from -6 to 6
- queries: bfloat16 [32768, 2048], P(('group', 'expert')), may hold values from -48 to 48
- span_kv: bfloat16 [2, 32768, 2048], P(None, ('group', 'expert')), may hold values from -4 to 4
- cache_kv: bfloat16 [2, 256, 2, 128, 2048], P(None, ('group', 'expert')), may hold values from -6 to 6
- seg_len: int32 [256, 2], P(('group', 'expert')), may hold values from 0 to 128, as said below
- o_rows: bfloat16 [2048, 2048], P('expert'), may hold values from -0.125 to 0.125
- norm_gain: float32 [2048], replicated, may hold values from 0.25 to 1.75
- routes: int32 [32768, 8], P(('group', 'expert')), may hold values from 0 to 31, all different within a row; in each aligned block of 128 rows (0 to 127, 128 to 255, ...) at most 48 rows name the same one
- route_wts: float32 [32768, 8], P(('group', 'expert')), may hold values from 0.05 to 0.6
- w_in: bfloat16 [32, 2048, 1024], P('expert'), may hold values from -0.125 to 0.125
- w_out: bfloat16 [32, 512, 2048], P('expert'), may hold values from -0.25 to 0.25
Outputs:
- layer_out: bfloat16 [32768, 2048], P(('group', 'expert'))
The draws below stay inside these ranges and needn't reach their ends.
Inputs may be any that keep to these rules, and one draw needn't show every extreme that they name: seg_len[d, 0] is 1 to 128; seg_len[d, 1] is 0 (the paired request is short) or 1 to 128; seg_len[0, 0] and seg_len[0, 1] are 128 and seg_len[1, 1] is 0. `routes`: each row names 8 different experts; among the 128 rows of one device no expert is named more than 48 times.
All inputs are finite; a program needn't handle non-finite values.
Results may differ from the reference program's by a relative error of at most 0.0053.
Values may be sent and summed in bfloat16 or wider, within the bound.
A program may use at most 128 MiB of HBM per device.

```python
import math
import jax
import jax.numpy as jnp
import numpy as np
from jax import lax

HEADS = 16
HD = 128
D = 2048
FF = 512
TOPK = 8
SPAN = 128
SEG = 128
EXPERTS = 32
CAP = 48
DEVS = 256
TOKENS = 32768
N_GROUP = 8
N_EXPERT = 32


def joint_rows(key):
    key_q, key_k, key_v = jax.random.split(jax.random.fold_in(key, 7), 3)
    keys_raw = jnp.clip(jax.random.normal(key_k, (TOKENS, D), jnp.float32), -4.0, 4.0)
    queries_raw = jnp.clip(jax.random.normal(key_q, (TOKENS, D), jnp.float32), -4.0, 4.0)
    values_raw = jnp.clip(jax.random.normal(key_v, (TOKENS, D), jnp.float32), -4.0, 4.0)
    return (queries_raw, keys_raw, values_raw)


def draw_queries(key, part):
    queries_raw, keys_raw, values_raw = joint_rows(key)
    return queries_raw.astype(jnp.bfloat16)


def draw_span_kv(key, part):
    queries_raw, keys_raw, values_raw = joint_rows(key)
    return jnp.stack([keys_raw, values_raw]).astype(jnp.bfloat16)


def draw_seg_len(key, part):
    key_own, key_long, key_part = jax.random.split(jax.random.fold_in(key, 11), 3)
    own_length = jax.random.randint(key_own, (DEVS,), 1, SEG + 1).astype(jnp.int32)
    own_length = own_length.at[0].set(SEG)
    is_long = jax.random.randint(key_long, (DEVS,), 0, 2).astype(jnp.int32)
    long_length = jax.random.randint(key_part, (DEVS,), 1, SEG + 1).astype(jnp.int32)
    second = jnp.where(is_long == 1, long_length, 0)
    second = second.at[0].set(SEG).at[1].set(0)
    return jnp.stack([own_length, second], axis=1).astype(jnp.int32)


def block_levels(own_key, shape, pieces, low, high):
    factor_of, own = 1.0, jax.random.fold_in(own_key, 6)
    for axis_at, parts in pieces:
        draws = jnp.exp(jax.random.uniform(jax.random.fold_in(own, axis_at), (parts,), jnp.float32, low / len(pieces), high / len(pieces)))
        factor_of = factor_of * jnp.repeat(draws, shape[axis_at] // parts).reshape([-1 if axis == axis_at else 1 for axis in range(len(shape))])
    return factor_of


def assign_block(own_key, own, number, rows, number_of, top, most, skew):
    sequence = jax.random.permutation(own_key, number_of)
    crowded, usual = load_shares(number_of, rows * top, most, skew, True), load_shares(number_of, rows * top, most, skew, False)
    places = jnp.arange(number_of)

    def named(lengths, offset_by):
        used = int((lengths > 0).sum())
        fixed = max(1, used // 4)
        passed = fixed + (places - fixed + offset_by * (used - fixed)) % max(1, number_of - fixed)
        return jnp.zeros((number_of,), jnp.int32).at[sequence[jnp.where(places < fixed, places, passed)]].set(jnp.asarray(lengths, jnp.int32))

    lengths = jnp.where(number % 4 == 0, named(crowded, number // 4), named(usual, number - number // 4 - 1))
    mixed = jax.random.permutation(jax.random.fold_in(own, 3), number_of)
    donor, receiver = mixed[0:number_of // 2 * 2:2], mixed[1:number_of // 2 * 2:2]
    room = jnp.minimum(lengths[donor] - 1, most - lengths[receiver]) // 2
    room = jnp.where((donor == sequence[0]) | (receiver == sequence[0]) | (lengths[receiver] == 0), 0, jnp.maximum(room, 0))
    passed = jax.random.randint(jax.random.fold_in(own, 4), (number_of // 2,), 0, 1 << 20) % (room + 1)
    lengths = lengths.at[donor].add(-passed).at[receiver].add(passed)
    members = jnp.searchsorted(jnp.cumsum(lengths), jnp.arange(rows * top), side="right").astype(jnp.int32)
    grid = members.reshape(top, rows).T
    grid = grid[jax.random.permutation(jax.random.fold_in(own, 1), rows)]
    offset_by = jax.random.randint(jax.random.fold_in(own, 2), (rows, 1), 0, top)
    return jnp.take_along_axis(grid, (jnp.arange(top)[None, :] + offset_by) % top, axis=1)


def load_shares(amount, total, bound, skew, full):
    loads = [(1 << 20) // math.isqrt(grade ** skew) + 1 for grade in range(1, amount + 1)]
    largest = bound if full else min(bound, max(-(-total // amount), total * loads[0] // sum(loads)))
    least = 1 if total - largest >= amount - 1 else 0
    holding, rest = [largest] + [least] * (amount - 1), total - largest - least * (amount - 1)
    while rest > 0:
        movable = [i for i in range(1, amount) if holding[i] < largest] or [i for i in range(1, amount) if holding[i] < bound]
        pool, budget = sum([loads[i] for i in movable]), rest
        for i in movable:
            addition = min(bound - holding[i], max(1, budget * loads[i] // pool), rest)
            holding[i] = holding[i] + addition
            rest = rest - addition
    return np.array(holding)


def scatter_about(own_key, extent, scale, limit, pieces=(), held_as=jnp.bfloat16):
    result = scale * jax.random.normal(own_key, extent, jnp.float32)
    if pieces:
        result = result * block_levels(own_key, extent, pieces, -0.22, 0.18)
    return jnp.clip(result, -limit, limit).astype(held_as)


def setup_inputs(seed: int = 0) -> dict:
    streams_of = jax.random.split(jax.random.key(seed), 12)
    resid = scatter_about(streams_of[0], (TOKENS, D), 1.0, 6.0, ((0, 256),))
    queries = draw_queries(jax.random.fold_in(streams_of[11], 71), 0)
    span_kv = draw_span_kv(jax.random.fold_in(streams_of[11], 71), 0)
    cache_kv = scatter_about(streams_of[3], (2, DEVS, 2, SEG, D), 1.0, 6.0, ((1, 256),))
    seg_len = draw_seg_len(jax.random.fold_in(streams_of[11], 71), 0)
    o_rows = scatter_about(streams_of[5], (D, D), D ** -0.5, 0.125, ((0, 32),))
    norm_gain = jnp.clip(1.0 + 0.15 * jax.random.normal(streams_of[6], (D,), jnp.float32), 0.25, 1.75)
    routes_keys = jax.random.split(jax.random.fold_in(streams_of[7], 1), TOKENS // SPAN)
    routes_turns = jax.random.permutation(jax.random.fold_in(streams_of[7], 3), TOKENS // SPAN)
    routes = jax.vmap(lambda own, number: assign_block(jax.random.fold_in(streams_of[7], 2), own, number, SPAN, EXPERTS, TOPK, CAP, 1))(routes_keys, routes_turns).reshape((TOKENS, TOPK))
    route_wts = jnp.clip(0.05 + 0.55 * jax.random.uniform(streams_of[8], (TOKENS, TOPK), jnp.float32) ** block_levels(streams_of[8], (TOKENS, TOPK), ((0, 256),), -0.2, 0.2), 0.05, 0.6)
    w_in = scatter_about(streams_of[9], (EXPERTS, D, 2 * FF), D ** -0.5, 0.125, ((0, 32),))
    w_out = scatter_about(streams_of[10], (EXPERTS, FF, D), FF ** -0.5, 0.25, ((0, 32),))
    return dict(resid=resid, queries=queries, span_kv=span_kv, cache_kv=cache_kv, seg_len=seg_len, o_rows=o_rows, norm_gain=norm_gain, routes=routes, route_wts=route_wts, w_in=w_in, w_out=w_out)


def attend(query_rows, key_rows, value_rows, valid_keys):
    q_heads = query_rows.astype(jnp.float32).reshape(-1, HEADS, HD)
    k_heads = key_rows.astype(jnp.float32).reshape(-1, HEADS, HD)
    v_heads = value_rows.astype(jnp.float32).reshape(-1, HEADS, HD)
    scores = jnp.einsum('chd,shd->hcs', q_heads, k_heads) * (1.0 / math.sqrt(HD))
    scores = jnp.where(valid_keys[None, None, :], scores, -1e+30)
    peak_score = lax.optimization_barrier(jnp.max(scores, axis=-1))
    expo = jnp.where(valid_keys[None, None, :], jnp.exp(scores - peak_score[..., None]), 0.0)
    totals = lax.optimization_barrier(jnp.sum(expo, axis=-1))
    probs_low = expo.astype(jnp.bfloat16).astype(jnp.float32)
    accum_out = jnp.einsum('hcs,shd->chd', probs_low, v_heads)
    return (peak_score, totals, accum_out)

def merge_parts(first, second):
    peak_a, total_a, accum_a = first
    peak_b, total_b, accum_b = second
    peak_both = jnp.maximum(peak_a, peak_b)
    scale_a = jnp.exp(peak_a - peak_both).T
    scale_b = jnp.exp(peak_b - peak_both).T
    numer = accum_a * scale_a[:, :, None] + accum_b * scale_b[:, :, None]
    denom = total_a.T * scale_a + total_b.T * scale_b
    merged = numer / denom[:, :, None]
    return merged.reshape(merged.shape[0], -1).astype(jnp.bfloat16)

def slot_of(route_rows):
    onehot = (route_rows[:, :, None] == jnp.arange(EXPERTS, dtype=jnp.int32)[None, None, :]).astype(jnp.int32)
    counts = lax.optimization_barrier(jnp.sum(onehot, axis=1))
    before = jnp.cumsum(counts, axis=0) - counts
    return lax.optimization_barrier(jnp.sum(onehot * before[:, None, :], axis=-1))

def expert_mlp(token_rows, weight_in, weight_out):
    joined = jnp.dot(token_rows, weight_in, preferred_element_type=jnp.float32)
    hidden = (jax.nn.silu(joined[:, :FF]) * joined[:, FF:]).astype(jnp.bfloat16)
    return jnp.dot(hidden, weight_out, preferred_element_type=jnp.float32).astype(jnp.bfloat16)

def reference(resid, queries, span_kv, cache_kv, seg_len, o_rows, norm_gain, routes, route_wts, w_in, w_out):
    query_blocks = queries.reshape(DEVS, SPAN, D)
    span_keys = span_kv[0].reshape(DEVS, SPAN, D)
    span_vals = span_kv[1].reshape(DEVS, SPAN, D)
    positions = jnp.arange(SEG, dtype=jnp.int32)

    def one_request(device):
        partner = jnp.bitwise_xor(device // N_EXPERT, 1) * N_EXPERT + device % N_EXPERT
        keys_a = jnp.concatenate([span_keys[device], cache_kv[0, device, 0]], axis=0)
        vals_a = jnp.concatenate([span_vals[device], cache_kv[1, device, 0]], axis=0)
        valid_a = jnp.concatenate([jnp.ones((SPAN,), bool), positions < seg_len[device, 0]])
        part_a = attend(query_blocks[device], keys_a, vals_a, valid_a)
        valid_b = positions < seg_len[partner, 1]
        part_b = attend(query_blocks[device], cache_kv[0, partner, 1], cache_kv[1, partner, 1], valid_b)
        return merge_parts(part_a, part_b)
    attended = lax.map(one_request, jnp.arange(DEVS, dtype=jnp.int32)).reshape(TOKENS, D)
    residual = resid.astype(jnp.float32) + jnp.dot(attended, o_rows, preferred_element_type=jnp.float32)
    normed = (residual * lax.rsqrt(lax.optimization_barrier(jnp.mean(residual * residual, axis=-1, keepdims=True)) + 1e-05) * norm_gain).astype(jnp.bfloat16)

    def one_group(group_id):
        start_row = (group_id * (N_EXPERT * SPAN)).astype(jnp.int32)
        group_acts = lax.dynamic_slice_in_dim(normed, start_row, N_EXPERT * SPAN, 0)
        group_resid = lax.dynamic_slice_in_dim(residual, start_row, N_EXPERT * SPAN, 0).reshape(N_EXPERT, SPAN, D)
        group_routes = lax.dynamic_slice_in_dim(routes, start_row, N_EXPERT * SPAN, 0).reshape(N_EXPERT, SPAN, TOPK)
        group_weights = lax.dynamic_slice_in_dim(route_wts, start_row, N_EXPERT * SPAN, 0).reshape(N_EXPERT, SPAN, TOPK)
        slot_ids = jax.vmap(slot_of)(group_routes)
        source = jnp.arange(N_EXPERT, dtype=jnp.int32)[:, None, None]
        buffer_pos = (group_routes * N_EXPERT + source) * CAP + slot_ids
        token_ids = jnp.broadcast_to(source * SPAN + jnp.arange(SPAN, dtype=jnp.int32)[None, :, None], buffer_pos.shape)
        slot_token = jnp.full((EXPERTS * N_EXPERT * CAP,), -1, jnp.int32).at[buffer_pos.reshape(-1)].set(token_ids.reshape(-1))
        token_rows = jnp.where((slot_token >= 0)[:, None], group_acts[jnp.maximum(slot_token, 0)], jnp.zeros((), jnp.bfloat16))
        token_rows = token_rows.reshape(EXPERTS, N_EXPERT * CAP, D)
        outputs = lax.map(lambda items: expert_mlp(items[0], items[1], items[2]), (token_rows, w_in, w_out))
        outputs = outputs.reshape(EXPERTS * N_EXPERT * CAP, D)
        expert_sum = jnp.zeros((N_EXPERT, SPAN, D), jnp.float32)
        for route_k in range(TOPK):
            picked = outputs[buffer_pos[:, :, route_k]].astype(jnp.float32)
            expert_sum = expert_sum + group_weights[:, :, route_k, None] * picked
        return (group_resid + expert_sum).astype(jnp.bfloat16).reshape(N_EXPERT * SPAN, D)
    layer_out = lax.map(one_group, jnp.arange(N_GROUP, dtype=jnp.int32))
    return layer_out.reshape(TOKENS, D)
```

```python
import functools
import math

import jax
import jax.numpy as jnp
from jax import lax
from jax.experimental import pallas as pl
from jax.experimental.pallas import tpu as pltpu
from jax.sharding import PartitionSpec as P

HEADS = 16
HD = 128
FF = 512
TOPK = 8
CAP = 48
NX, NY, NZ = 4, 4, 8
EXPERTS = NY * NZ
D = 2048
SPAN = 128
HALF = D // 2
MESH = pl.DeviceIdType.MESH
F32, BF16 = jnp.float32, jnp.bfloat16


def layer_kernel(
    small, gain, resid, queries, span_kv, cache_kv, o_rows, w_in, w_out, out,
    qb, kv, segs, obuf, att, pr, prs, res, tok, mt, wi, wo, xs, hb, rbuf,
    loc, osem_s, osem_r, zsem_s, zsem_r, msem_s, msem_r, isem_s, isem_r, xsem_s, xsem_r,
    usem_s, usem_r, csem_s, csem_r, tsem_s, tsem_r, rsem_s, rsem_r,
):
    g, e = lax.axis_index("group"), lax.axis_index("expert")
    x, c = g // 2, g % 2
    y, z = e // NZ, e % NZ
    f = 1 - 2 * c

    def ring(v, by, n):
        return lax.rem(v + by + 2 * n, n)

    def at(dx=0, dc=0, dy=0, dz=0):
        return (ring(x, dx, NX) * 2 + ring(c, dc, 2), ring(y, dy, NY) * NZ + ring(z, dz, NZ))

    sib = at(dc=1)
    peers = [sib]
    for way in (1, -1):
        peers += [at(dx=way), at(dy=way), at(dz=way)]
    barrier = pltpu.get_barrier_semaphore()
    for peer in peers:
        pl.semaphore_signal(barrier, inc=1, device_id=peer, device_id_type=MESH)

    def remote(src, dst, send, recv, peer):
        return pltpu.make_async_remote_copy(
            src_ref=src, dst_ref=dst, send_sem=send, recv_sem=recv, device_id=peer, device_id_type=MESH
        )

    local = [
        pltpu.make_async_copy(queries, qb, loc.at[0]),
        pltpu.make_async_copy(span_kv, kv.at[:, 0], loc.at[1]),
        pltpu.make_async_copy(cache_kv.at[:, 0, 0], kv.at[:, 1], loc.at[2]),
        pltpu.make_async_copy(o_rows.at[:, pl.ds(c * HALF, HALF)], obuf.at[y, z], loc.at[3]),
        pltpu.make_async_copy(w_in.at[0], wi.at[y], loc.at[4]),
        pltpu.make_async_copy(w_out.at[0], wo.at[y], loc.at[5]),
    ]
    for copy in (local[3], local[0], local[1], local[2]):
        copy.start()
    pl.semaphore_wait(barrier, len(peers))

    started = []

    def go(copy):
        copy.start()
        started.append(copy)
        return copy

    c_kv = go(remote(cache_kv.at[:, 0, 1], kv.at[:, 2], csem_s.at[0], csem_r.at[0], sib))
    c_seg = go(remote(small.at[pl.ds(16, 8)], segs, csem_s.at[1], csem_r.at[1], sib))

    def ring_slots(me, n):
        return [ring(me, -k * f, n) for k in range(n // 2 + 1)], [ring(me, k * f, n) for k in range(n // 2)]

    ys_f, ys_b = ring_slots(y, NY)
    zs_f, zs_b = ring_slots(z, NZ)
    xs_f, xs_b = ring_slots(x, NX)
    y_f, y_b = at(dy=f), at(dy=-f)
    z_f, z_b = at(dz=f), at(dz=-f)
    x_f, x_b = at(dx=f), at(dx=-f)

    class Ring:
        def __init__(self, n, view, own, slots_f, slots_b, to_f, to_b, ss, rs, base=0):
            self.n, self.view, self.slots_f, self.slots_b = n, view, slots_f, slots_b
            self.to_f, self.to_b, self.ss, self.rs, self.base = to_f, to_b, ss, rs, base
            self.own = own
            self.f, self.b = {}, {}

        def put_f(self, k):
            src = self.own if k == 0 else self.view(self.slots_f[k])
            i = self.base + k
            self.f[k + 1] = go(remote(src, self.view(self.slots_f[k]), self.ss.at[i], self.rs.at[i], self.to_f))

        def put_b(self, k):
            src = self.own if k == 0 else self.view(self.slots_b[k])
            i = self.base + self.n // 2 + k
            self.b[k + 1] = go(remote(src, self.view(self.slots_b[k]), self.ss.at[i], self.rs.at[i], self.to_b))

        def start(self):
            self.put_f(0)
            self.put_b(0)

        def step_f(self, k):
            self.f[k].wait_recv()
            if k < self.n // 2:
                self.put_f(k)

        def step_b(self, k):
            self.b[k].wait_recv()
            if k < self.n // 2 - 1:
                self.put_b(k)

    o_y = Ring(NY, lambda s: obuf.at[s, z], o_rows.at[:, pl.ds(c * HALF, HALF)], ys_f, ys_b, y_f, y_b, osem_s, osem_r)
    o_y.start()

    lanes_e = lax.broadcasted_iota(jnp.int32, (EXPERTS, SPAN), 0).astype(F32)
    hit = jnp.zeros((EXPERTS, SPAN), F32)
    wts = jnp.zeros((EXPERTS, SPAN), F32)
    for k in range(TOPK):
        same = lanes_e == small[k : k + 1, :]
        hit = jnp.where(same, 1.0, hit)
        wts = jnp.where(same, small[8 + k : 9 + k, :], wts)
    rows_t = lax.broadcasted_iota(jnp.int32, (SPAN, SPAN), 0)
    cols_t = lax.broadcasted_iota(jnp.int32, (SPAN, SPAN), 1)
    earlier = (rows_t < cols_t).astype(F32).astype(BF16)
    before = jnp.dot(hit.astype(BF16), earlier, preferred_element_type=F32)
    pos = jnp.where(hit > 0.5, before, -1.0)
    for yy in range(NY):
        for zz in range(NZ):
            j = yy * NZ + zz
            mt[z, zz, yy : yy + 1, :] = pos[j : j + 1, :]
            mt[z, zz, 4 + yy : 5 + yy, :] = wts[j : j + 1, :]
    m_z = Ring(NZ, lambda s: mt.at[s], mt.at[z], zs_f, zs_b, z_f, z_b, msem_s, msem_r)
    m_z.start()

    i_y = Ring(NY, lambda s: wi.at[s, x, c], w_in.at[0, x, c], ys_f, ys_b, y_f, y_b, isem_s, isem_r)
    u_y = Ring(NY, lambda s: wo.at[s, c], w_out.at[0, c], ys_f, ys_b, y_f, y_b, usem_s, usem_r)
    others = [ys_f[1], ys_b[1], ys_f[2]]
    i_x = [
        Ring(NX, functools.partial(lambda yy, s: wi.at[yy, s, c], yy), wi.at[yy, x, c], xs_f, xs_b, x_f, x_b, xsem_s, xsem_r, base=3 * i)
        for i, yy in enumerate(others)
    ]
    w_sib = {}

    def share_in(i):
        yy = others[i]
        w_sib[i] = go(remote(wi.at[yy, :, c], wi.at[yy, :, c], csem_s.at[4 + i], csem_r.at[4 + i], sib))

    def share_out(i):
        yy = others[i]
        w_sib[3 + i] = go(remote(wo.at[yy, c], wo.at[yy, c], csem_s.at[7 + i], csem_r.at[7 + i], sib))

    for copy in local[:3]:
        copy.wait()
    o_y.step_f(1)
    o_y.step_b(1)
    i_y.start()
    local[4].start()
    local[5].start()
    c_kv.wait_recv()
    c_seg.wait_recv()

    lane = lax.broadcasted_iota(jnp.int32, (1, SPAN), 1).astype(F32)
    valid = jnp.concatenate(
        [jnp.ones((1, SPAN), F32), (lane < small[16:17, :]).astype(F32), (lane < segs[1:2, :]).astype(F32)], axis=1
    )

    def head(h, carry):
        cols = pl.ds(pl.multiple_of(h * HD, HD), HD)
        q = qb[:, cols]
        keys = kv[0, :, :, cols].reshape(3 * SPAN, HD)
        vals = kv[1, :, :, cols].reshape(3 * SPAN, HD)
        s = lax.dot_general(q, keys, (((1,), (1,)), ((), ())), preferred_element_type=F32) * (1.0 / math.sqrt(HD))
        s = jnp.where(valid > 0.5, s, -1e30)
        m = jnp.max(s, axis=-1, keepdims=True)
        w = jnp.exp(s - m)
        total = jnp.sum(w, axis=-1, keepdims=True)
        a = jnp.dot(w.astype(BF16), vals, preferred_element_type=F32)
        att[c, :, cols] = (a / total).astype(BF16)
        return carry

    def heads(lo, hi):
        lax.fori_loop(lo, hi, head, 0)

    o_z = Ring(NZ, lambda s: obuf.at[:, s], obuf.at[:, z], zs_f, zs_b, z_f, z_b, zsem_s, zsem_r)
    heads(0, 4)
    o_y.step_f(2)
    local[3].wait()
    o_z.start()
    m_z.step_f(1)
    m_z.step_b(1)
    heads(4, 8)
    m_z.step_f(2)
    m_z.step_b(2)
    heads(8, 12)
    m_z.step_f(3)
    m_z.step_b(3)
    heads(12, 16)
    c_att = go(remote(att.at[c], att.at[c], csem_s.at[2], csem_r.at[2], sib))
    i_y.step_f(1)
    i_y.step_b(1)
    i_x[0].start()
    i_x[1].start()
    u_y.start()
    o_z.step_f(1)
    o_z.step_b(1)
    i_y.step_f(2)
    i_x[2].start()
    o_z.step_f(2)
    o_z.step_b(2)
    i_x[0].step_f(1)
    i_x[0].step_b(1)
    u_y.step_f(1)
    u_y.step_b(1)
    share_out(0)
    share_out(1)
    i_x[1].step_f(1)
    i_x[1].step_b(1)
    o_z.step_f(3)
    o_z.step_b(3)
    m_z.step_f(4)
    c_att.wait_recv()
    i_x[2].step_f(1)
    i_x[2].step_b(1)
    o_z.step_f(4)

    both = att[...].reshape(2 * SPAN, D)

    def project(n, carry):
        cols = pl.ds(pl.multiple_of(n * 256, 256), 256)
        got = jnp.dot(both, obuf[:, :, :, cols].reshape(D, 256), preferred_element_type=F32)
        prs[:, :, cols] = got.reshape(2, SPAN, 256)
        return carry

    lax.fori_loop(0, HALF // 256, project, 0)
    c_pr = go(remote(prs.at[1 - c], pr, csem_s.at[3], csem_r.at[3], sib))
    pltpu.sync_copy(resid, qb)
    c_pr.wait_recv()
    mine = prs[c]
    theirs = pr[...]
    first = c == 0
    low = qb[:, :HALF].astype(F32) + jnp.where(first, mine, theirs)
    high = qb[:, HALF:].astype(F32) + jnp.where(first, theirs, mine)
    squares = jnp.sum(low * low, axis=-1, keepdims=True) + jnp.sum(high * high, axis=-1, keepdims=True)
    scale = lax.rsqrt(squares * (1.0 / D) + 1e-05)
    res[:, :HALF] = low
    res[:, HALF:] = high
    tok[z, :, :HALF] = (low * scale * gain[:, :HALF]).astype(BF16)
    tok[z, :, HALF:] = (high * scale * gain[:, HALF:]).astype(BF16)
    t_z = Ring(NZ, lambda s: tok.at[s], tok.at[z], zs_f, zs_b, z_f, z_b, tsem_s, tsem_r)
    t_z.start()

    slot = lax.broadcasted_iota(jnp.int32, (CAP, SPAN), 0).astype(F32)

    def place(src, i):
        pick = jnp.concatenate(
            [jnp.where(slot == mt[src, z, yy : yy + 1, :], 1.0, 0.0) for yy in range(NY)], axis=0
        ).astype(BF16)

        def tile(n, carry):
            cols = pl.ds(pl.multiple_of(n * 512, 512), 512)
            rows = jnp.dot(pick, tok[src, :, cols], preferred_element_type=F32).astype(BF16)
            for yy in range(NY):
                xs[yy, i * CAP : (i + 1) * CAP, cols] = rows[yy * CAP : (yy + 1) * CAP]
            return carry

        lax.fori_loop(0, D // 512, tile, 0)

    def mlp(yy, lo, hi):
        part = slice(lo * CAP, hi * CAP)
        count = (hi - lo) * CAP

        def up(n, carry):
            gate = pl.ds(pl.multiple_of(n * 256, 256), 256)
            lift = pl.ds(pl.multiple_of(FF + n * 256, 256), 256)
            rows = xs[yy, part, :]
            a = jnp.dot(rows, wi[yy, :, :, :, gate].reshape(D, 256), preferred_element_type=F32)
            b = jnp.dot(rows, wi[yy, :, :, :, lift].reshape(D, 256), preferred_element_type=F32)
            hb[:count, gate] = (a * (1.0 / (1.0 + jnp.exp(-a))) * b).astype(BF16)
            return carry

        lax.fori_loop(0, FF // 256, up, 0)

        def down(n, carry):
            cols = pl.ds(pl.multiple_of(n * 512, 512), 512)
            xs[yy, part, cols] = jnp.dot(
                hb[:count, :], wo[yy, :, :, cols].reshape(FF, 512), preferred_element_type=F32
            ).astype(BF16)
            return carry

        lax.fori_loop(0, D // 512, down, 0)

    def combine(src, i, store):
        w = jnp.concatenate(
            [
                jnp.where(slot == mt[src, z, yy : yy + 1, :], mt[src, z, 4 + yy : 5 + yy, :], 0.0)
                for yy in range(NY)
            ],
            axis=0,
        )
        high = w.astype(BF16)
        low = (w - high.astype(F32)).astype(BF16)
        dims = (((0,), (0,)), ((), ()))

        def tile(n, carry):
            cols = pl.ds(pl.multiple_of(n * 512, 512), 512)
            rows = xs[:, i * CAP : (i + 1) * CAP, cols].reshape(NY * CAP, 512)
            got = lax.dot_general(high, rows, dims, preferred_element_type=F32)
            got += lax.dot_general(low, rows, dims, preferred_element_type=F32)
            store(cols, got)
            return carry

        lax.fori_loop(0, D // 512, tile, 0)

    order = [y] + others
    sources = [z, zs_f[1], zs_b[1], zs_f[2], zs_b[2], zs_f[3], zs_b[3], zs_f[4]]

    place(sources[0], 0)
    local[4].wait()
    local[5].wait()
    u_y.step_f(2)
    share_out(2)
    i_x[0].step_f(2)
    share_in(0)
    t_z.step_f(1)
    t_z.step_b(1)
    place(sources[1], 1)
    place(sources[2], 2)
    i_x[1].step_f(2)
    share_in(1)
    t_z.step_f(2)
    t_z.step_b(2)
    i_x[2].step_f(2)
    share_in(2)
    place(sources[3], 3)
    place(sources[4], 4)
    mlp(y, 0, 5)
    for i, came in enumerate((1, 0, 2)):
        w_sib[came].wait_recv()
        w_sib[3 + came].wait_recv()
        mlp(others[i], 0, 5)
    t_z.step_f(3)
    t_z.step_b(3)
    place(sources[5], 5)
    place(sources[6], 6)

    def mlp_all(lo, hi):
        def one(i, carry):
            mlp(ring(y, i, NY), lo, hi)
            return carry

        lax.fori_loop(0, NY, one, 0)

    mlp_all(5, 7)

    for copies in (t_z.f, t_z.b):
        for copy in copies.values():
            copy.wait_send()

    back_f, back_b = {}, {}

    def send_f(k):
        i = k - 1
        back_f[k - 1] = go(remote(tok.at[zs_f[k]], rbuf.at[i], rsem_s.at[i], rsem_r.at[i], z_b))

    def send_b(k):
        i = 4 + k - 1
        back_b[k - 1] = go(remote(tok.at[zs_b[k]], rbuf.at[i], rsem_s.at[i], rsem_r.at[i], z_f))

    def only(dest):
        def store(cols, got):
            tok[dest, :, cols] = got.astype(BF16)

        return store

    def added(dest, slot_at):
        def store(cols, got):
            tok[dest, :, cols] = (got + rbuf[slot_at, :, cols].astype(F32)).astype(BF16)

        return store

    combine(zs_b[3], 6, only(zs_b[3]))
    send_b(3)
    t_z.step_f(4)
    place(sources[7], 7)
    mlp_all(7, 8)
    combine(zs_f[4], 7, only(zs_f[4]))
    send_f(4)

    def hop_b(k, i):
        back_b[k].wait_recv()
        combine(zs_b[k], i, added(zs_b[k], 4 + k))
        send_b(k)

    def hop_f(k, i):
        back_f[k].wait_recv()
        combine(zs_f[k], i, added(zs_f[k], k))
        send_f(k)

    hop_b(2, 4)
    hop_f(3, 5)
    hop_b(1, 2)
    hop_f(2, 3)
    hop_f(1, 1)

    def own(cols, got):
        res[:, cols] = res[:, cols] + got

    combine(z, 0, own)
    back_b[0].wait_recv()
    back_f[0].wait_recv()
    out[...] = (res[...] + rbuf[0].astype(F32) + rbuf[4].astype(F32)).astype(BF16)
    waited = {id(copy) for ring_of in (t_z.f, t_z.b) for copy in ring_of.values()}
    for copy in started:
        if id(copy) not in waited:
            copy.wait_send()


def shards(resid, queries, span_kv, cache_kv, seg_len, o_rows, norm_gain, routes, route_wts, w_in, w_out):
    lens = jnp.broadcast_to(seg_len.astype(F32).T, (2, SPAN))
    small = jnp.concatenate([routes.astype(F32).T, route_wts.T, lens, jnp.zeros((6, SPAN), F32)], axis=0)
    hbm = pl.BlockSpec(memory_space=pl.ANY)
    vmem = pl.BlockSpec(memory_space=pltpu.VMEM)
    dma = pltpu.SemaphoreType.DMA
    return pl.pallas_call(
        layer_kernel,
        out_shape=jax.ShapeDtypeStruct((SPAN, D), BF16),
        in_specs=[vmem, vmem] + [hbm] * 7,
        out_specs=vmem,
        scratch_shapes=[
            pltpu.VMEM((SPAN, D), BF16),
            pltpu.VMEM((2, 3, SPAN, D), BF16),
            pltpu.VMEM((8, SPAN), F32),
            pltpu.VMEM((NY, NZ, D // EXPERTS, HALF), BF16),
            pltpu.VMEM((2, SPAN, D), BF16),
            pltpu.VMEM((SPAN, HALF), F32),
            pltpu.VMEM((2, SPAN, HALF), F32),
            pltpu.VMEM((SPAN, D), F32),
            pltpu.VMEM((NZ, SPAN, D), BF16),
            pltpu.VMEM((NZ, NZ, 8, SPAN), F32),
            pltpu.VMEM((NY, NX, 2, D // 8, 2 * FF), BF16),
            pltpu.VMEM((NY, 2, FF // 2, D), BF16),
            pltpu.VMEM((NY, NZ * CAP, D), BF16),
            pltpu.VMEM((5 * CAP, FF), BF16),
            pltpu.VMEM((7, SPAN, D), BF16),
            dma((6,)),
            dma((3,)), dma((3,)),
            dma((7,)), dma((7,)),
            dma((7,)), dma((7,)),
            dma((3,)), dma((3,)),
            dma((9,)), dma((9,)),
            dma((3,)), dma((3,)),
            dma((10,)), dma((10,)),
            dma((7,)), dma((7,)),
            dma((7,)), dma((7,)),
        ],
        compiler_params=pltpu.CompilerParams(collective_id=0, has_side_effects=True, vmem_limit_bytes=62 << 20),
    )(
        small,
        norm_gain.reshape(1, D),
        resid,
        queries,
        span_kv,
        cache_kv,
        o_rows,
        w_in.reshape(1, NX, 2, D // 8, 2 * FF),
        w_out.reshape(1, 2, FF // 2, D),
    )


def solution(mesh):
    rows = P(("group", "expert"), None)
    placed = (
        rows,
        rows,
        P(None, ("group", "expert"), None),
        P(None, ("group", "expert"), None, None, None),
        rows,
        P("expert", None),
        P(),
        rows,
        rows,
        P("expert", None, None),
        P("expert", None, None),
    )
    return jax.shard_map(shards, mesh=mesh, in_specs=placed, out_specs=rows, check_vma=False)
```

```python
import functools
import math

import jax
import jax.numpy as jnp
from jax import lax
from jax.experimental import pallas as pl
from jax.experimental.pallas import tpu as pltpu
from jax.sharding import PartitionSpec as P

HEADS = 16
HD = 128
FF = 512
TOPK = 8
CAP = 48
NX, NY, NZ = 4, 4, 8
EXPERTS = NY * NZ
D = 2048
SPAN = 128
HALF = D // 2
OX = 128
OZ = HALF - NX * OX
WY = 512
PIECE = 512
MESH = pl.DeviceIdType.MESH
F32, BF16 = jnp.float32, jnp.bfloat16


def layer_kernel(
    routes, route_wts, seg_len, gain, resid, queries, span_kv, cache_kv, o_rows, w_in, w_out, out,
    qb, kv, segs, seg_out, obuf, att, pr, prs, res, tok, mine_t, mt, wiy, wix, wo, xs, hb, rbuf, loc, sent, came,
):
    g, e = lax.axis_index("group"), lax.axis_index("expert")
    x, c = g // 2, g % 2
    y, z = e // NZ, e % NZ
    f = 1 - 2 * c

    def ring(v, by, n):
        return lax.rem(v + by + 2 * n, n)

    def at(dx=0, dc=0, dy=0, dz=0):
        return (ring(x, dx, NX) * 2 + ring(c, dc, 2), ring(y, dy, NY) * NZ + ring(z, dz, NZ))

    sib = at(dc=1)
    x_peers = [at(dx=k) for k in (1, NX - 1, 2)]
    y_peers = [at(dy=k) for k in (1, NY - 1, 2)]
    z_peers = [at(dz=k) for k in range(1, NZ)]
    peers = [sib] + x_peers + y_peers + z_peers
    barrier = pltpu.get_barrier_semaphore()
    for peer in peers:
        pl.semaphore_signal(barrier, inc=1, device_id=peer, device_id_type=MESH)

    half = c * HALF
    local = [
        pltpu.make_async_copy(o_rows.at[:, pl.ds(half, OZ)], obuf.at[0, z, :, pl.ds(0, OZ)], loc.at[0]),
        pltpu.make_async_copy(o_rows.at[:, pl.ds(half + OZ + x * OX, OX)], obuf.at[0, z, :, pl.ds(OZ, OX)], loc.at[1]),
        pltpu.make_async_copy(queries, qb, loc.at[2]),
        pltpu.make_async_copy(span_kv, kv.at[:, 0], loc.at[3]),
        pltpu.make_async_copy(cache_kv.at[:, 0, 0], kv.at[:, 1], loc.at[4]),
        pltpu.make_async_copy(w_in.at[:, pl.ds(0, WY)], wiy.at[pl.ds(y, 1)], loc.at[5]),
        pltpu.make_async_copy(w_in.at[:, pl.ds(WY, D - WY)], wix.at[pl.ds(y, 1)], loc.at[6]),
        pltpu.make_async_copy(w_out, wo.at[pl.ds(y, 1)], loc.at[7]),
    ]
    for copy in local[:5]:
        copy.start()
    seg_out[...] = jnp.broadcast_to(seg_len[:, 1:2].astype(F32), seg_out.shape)
    pl.semaphore_wait(barrier, len(peers))

    started, used, done = [], [0], set()

    def remote(src, dst, peer, slot=None):
        i = used[0] if slot is None else slot
        used[0] += slot is None
        copy = pltpu.make_async_remote_copy(
            src_ref=src, dst_ref=dst, send_sem=sent.at[i], recv_sem=came.at[i], device_id=peer, device_id_type=MESH
        )
        copy.start()
        started.append(copy)
        return copy

    def gone(copy):
        copy.wait_send()
        done.add(id(copy))

    def slots(n):
        i = used[0]
        used[0] += n
        return i

    def ring_slots(me, n):
        return [ring(me, -k * f, n) for k in range(n // 2 + 1)], [ring(me, k * f, n) for k in range(n // 2)]

    ys_f, ys_b = ring_slots(y, NY)
    zs_f, zs_b = ring_slots(z, NZ)
    xs_f, xs_b = ring_slots(x, NX)
    to_y, to_z, to_x = (at(dy=f), at(dy=-f)), (at(dz=f), at(dz=-f)), (at(dx=f), at(dx=-f))

    class Ring:
        def __init__(self, n, view, slots_f, slots_b, to, own=None, view_to=None):
            self.n, self.view, self.slots_f, self.slots_b, self.to = n, view, slots_f, slots_b, to
            self.own = view(slots_f[0]) if own is None else own
            self.view_to = view_to or (lambda s, way: view(s))
            self.base = slots(n - 1)
            self.f, self.b = {}, {}

        def put_f(self, k):
            src = self.own if k == 0 else self.view(self.slots_f[k])
            self.f[k + 1] = remote(src, self.view_to(self.slots_f[k], f), self.to[0], self.base + k)

        def put_b(self, k):
            src = self.own if k == 0 else self.view(self.slots_b[k])
            self.b[k + 1] = remote(src, self.view_to(self.slots_b[k], -f), self.to[1], self.base + self.n // 2 + k)

        def start(self):
            self.put_f(0)
            self.put_b(0)

        def step_f(self, k):
            self.f[k].wait_recv()
            if k < self.n // 2:
                self.put_f(k)

        def step_b(self, k):
            self.b[k].wait_recv()
            if k < self.n // 2 - 1:
                self.put_b(k)

        def step(self, k):
            self.step_f(k)
            if k < self.n // 2:
                self.step_b(k)

    zx = pl.ds(0, OZ + OX)
    local[0].wait()
    local[1].wait()
    o_y = [
        remote(obuf.at[0, z, :, zx], obuf.at[NY - k, z, :, zx], peer) for k, peer in zip((1, NY - 1, 2), y_peers)
    ]
    c_kv = remote(cache_kv.at[:, 0, 1], kv.at[:, 2], sib)
    c_seg = remote(seg_out, segs, sib)

    chunks = [pl.ds(OZ, OX)] + [pl.ds(k * (OZ // 2), OZ // 2) for k in range(2)]
    o_z = [Ring(NZ, functools.partial(lambda cols, s: obuf.at[:, s, :, cols], cols), zs_f, zs_b, to_z) for cols in chunks]
    o_x = []

    def spread(zz):
        for k, peer in zip((1, NX - 1, 2), x_peers):
            there = pl.ds(OZ + (NX - k) * OX, OX)
            o_x.append(remote(obuf.at[:, zz, :, chunks[0]], obuf.at[:, zz, :, there], peer))

    others = [ys_f[1], ys_b[1], ys_f[2]]
    deep = (D - WY) // 8

    def shard(s, start=0):
        return pl.ds(pl.multiple_of(start + (c * NX + s) * deep, 16), deep)

    def core_half(n):
        return pl.ds(pl.multiple_of(c * (n // 2), 16), n // 2)

    i_y = Ring(NY, lambda s: wix.at[s, shard(x)], ys_f, ys_b, to_y, own=w_in.at[0, shard(x, WY)])
    v_y = Ring(NY, lambda s: wiy.at[s, core_half(WY)], ys_f, ys_b, to_y, own=w_in.at[0, core_half(WY)])
    u_y = Ring(NY, lambda s: wo.at[s, core_half(FF)], ys_f, ys_b, to_y, own=w_out.at[0, core_half(FF)])
    i_x = [
        Ring(NX, functools.partial(lambda yy, s: wix.at[yy, shard(s)], yy), xs_f, xs_b, to_x)
        for yy in others
    ]
    w_sib, w_at = {}, slots(9)

    def share(i, what):
        yy = others[i]
        part = {"x": wix.at[yy, core_half(D - WY)], "y": wiy.at[yy, core_half(WY)], "o": wo.at[yy, core_half(FF)]}[what]
        w_sib[i, what] = remote(part, part, sib, w_at + 3 * i + "xyo".index(what))

    def have(i):
        for what in "yox":
            w_sib[(1, 0, 2)[i], what].wait_recv()

    lanes_e = lax.broadcasted_iota(jnp.int32, (EXPERTS, SPAN), 0).astype(F32)
    hit = jnp.zeros((EXPERTS, SPAN), F32)
    wts = jnp.zeros((EXPERTS, SPAN), F32)
    for k in range(TOPK):
        same = lanes_e == routes[k : k + 1, :].astype(F32)
        hit = jnp.where(same, 1.0, hit)
        wts = jnp.where(same, route_wts[k : k + 1, :], wts)
    rows_t = lax.broadcasted_iota(jnp.int32, (SPAN, SPAN), 0)
    cols_t = lax.broadcasted_iota(jnp.int32, (SPAN, SPAN), 1)
    earlier = (rows_t < cols_t).astype(F32).astype(BF16)
    before = jnp.dot(hit.astype(BF16), earlier, preferred_element_type=F32)
    pos = jnp.where(hit > 0.5, before, -1.0)
    for yy in range(NY):
        for zz in range(NZ):
            j = yy * NZ + zz
            mine_t[zz, yy : yy + 1, :] = pos[j : j + 1, :]
            mine_t[zz, 4 + yy : 5 + yy, :] = wts[j : j + 1, :]
    mt[z] = mine_t[z]
    metas = []
    for k in range(1, NZ):
        metas.append(remote(mine_t.at[ring(z, k, NZ)], mt.at[z], z_peers[k - 1]))

    for copy in local[2:5]:
        copy.wait()
    c_kv.wait_recv()
    c_seg.wait_recv()

    lane = lax.broadcasted_iota(jnp.int32, (1, SPAN), 1).astype(F32)
    valid = jnp.concatenate(
        [jnp.ones((1, SPAN), F32), (lane < seg_len[:, 0:1].astype(F32)).astype(F32), (lane < segs[0:1, :]).astype(F32)], axis=1
    )

    def head(h, carry):
        cols = pl.ds(pl.multiple_of(h * HD, HD), HD)
        q = qb[:, cols]
        keys = kv[0, :, :, cols].reshape(3 * SPAN, HD)
        vals = kv[1, :, :, cols].reshape(3 * SPAN, HD)
        s = lax.dot_general(q, keys, (((1,), (1,)), ((), ())), preferred_element_type=F32) * (1.0 / math.sqrt(HD))
        s = jnp.where(valid > 0.5, s, -1e30)
        m = jnp.max(s, axis=-1, keepdims=True)
        w = jnp.exp(s - m)
        total = jnp.sum(w, axis=-1, keepdims=True)
        a = jnp.dot(w.astype(BF16), vals, preferred_element_type=F32)
        att[c, :, cols] = (a / total).astype(BF16)
        return carry

    def heads(lo, hi):
        lax.fori_loop(lo, hi, head, 0)

    heads(0, 4)
    for copy in o_y:
        copy.wait_recv()
    for o in o_z:
        o.start()
    spread(z)
    i_y.start()
    for copy in local[5:]:
        copy.start()
    heads(4, 12)
    o_z[0].step(1)
    spread(zs_f[1])
    spread(zs_b[1])
    heads(12, 16)
    c_att = remote(att.at[c], att.at[c], sib)
    load = pltpu.make_async_copy(resid, qb, loc.at[2])
    load.start()
    o_z[1].step(1)
    o_z[2].step(1)
    o_z[0].step(2)
    spread(zs_f[2])
    spread(zs_b[2])
    i_y.step(1)
    v_y.start()
    u_y.start()
    o_z[1].step(2)
    o_z[2].step(2)
    o_z[0].step(3)
    spread(zs_f[3])
    spread(zs_b[3])
    i_y.step_f(2)
    o_z[1].step(3)
    o_z[2].step(3)
    o_z[0].step_f(4)
    spread(zs_f[4])
    i_x[0].start()
    i_x[1].start()
    for copy in metas:
        copy.wait_recv()
    c_att.wait_recv()
    o_z[1].step_f(4)
    o_z[2].step_f(4)
    for copy in o_x:
        copy.wait_recv()

    def columns(n):
        cols = pl.ds(pl.multiple_of(n * 256, 256), 256)
        total = jnp.zeros((2 * SPAN, 256), F32)
        for r in range(NY):
            depth = pl.ds(pl.multiple_of(ring(y, r, NY) * (D // NY), D // NY), D // NY)
            rows = att[:, :, depth].reshape(2 * SPAN, D // NY)
            total += jnp.dot(rows, obuf[r, :, :, cols].reshape(D // NY, 256), preferred_element_type=F32)
        return total.reshape(2, SPAN, 256)

    def project_z(n, carry):
        prs[:, :, pl.ds(pl.multiple_of(n * 256, 256), 256)] = columns(n)
        return carry

    def project_x(n):
        got = columns(OZ // 256 + n)
        for i in range(2):
            spot = pl.ds(pl.multiple_of(OZ + ring(x, 2 * n + i, NX) * OX, OX), OX)
            prs[:, :, spot] = got[:, :, i * OX : (i + 1) * OX]

    lax.fori_loop(0, OZ // 256, project_z, 0)
    for n in range(NX * OX // 256):
        project_x(n)
    c_pr = remote(prs.at[1 - c], pr, sib)
    load.wait()
    c_pr.wait_recv()
    mine = prs[c]
    theirs = pr[...]
    first = c == 0
    low = qb[:, :HALF].astype(F32) + jnp.where(first, mine, theirs)
    high = qb[:, HALF:].astype(F32) + jnp.where(first, theirs, mine)
    squares = jnp.sum(low * low, axis=-1, keepdims=True) + jnp.sum(high * high, axis=-1, keepdims=True)
    scale = lax.rsqrt(squares * (1.0 / D) + 1e-05)
    tok[z, :, :HALF] = (low * scale * gain[:, :HALF]).astype(BF16)
    t_z = [Ring(NZ, functools.partial(lambda j, s: tok.at[s, :, pl.ds(j * HALF, HALF)], j), zs_f, zs_b, to_z) for j in range(2)]
    t_z[0].start()
    tok[z, :, HALF:] = (high * scale * gain[:, HALF:]).astype(BF16)
    t_z[1].start()
    res[:, :HALF] = low
    res[:, HALF:] = high

    slot = lax.broadcasted_iota(jnp.int32, (CAP, SPAN), 0).astype(F32)

    def place(src, i):
        pick = jnp.concatenate(
            [jnp.where(slot == mt[src, yy : yy + 1, :], 1.0, 0.0) for yy in range(NY)], axis=0
        ).astype(BF16)

        def tile(n, carry):
            cols = pl.ds(pl.multiple_of(n * 512, 512), 512)
            rows = jnp.dot(pick, tok[src, :, cols], preferred_element_type=F32).astype(BF16)
            for yy in range(NY):
                xs[yy, i * CAP : (i + 1) * CAP, cols] = rows[yy * CAP : (yy + 1) * CAP]
            return carry

        lax.fori_loop(0, D // 512, tile, 0)

    def mlp(yy, lo, hi):
        part = slice(lo * CAP, hi * CAP)
        count = (hi - lo) * CAP

        def up(n, carry):
            gate = pl.ds(pl.multiple_of(n * 256, 256), 256)
            lift = pl.ds(pl.multiple_of(FF + n * 256, 256), 256)

            def times(cols):
                got = jnp.dot(xs[yy, part, :WY], wiy[yy, :, cols], preferred_element_type=F32)
                return got + jnp.dot(xs[yy, part, WY:], wix[yy, :, cols], preferred_element_type=F32)

            a, b = times(gate), times(lift)
            hb[:count, gate] = (a * (1.0 / (1.0 + jnp.exp(-a))) * b).astype(BF16)
            return carry

        lax.fori_loop(0, FF // 256, up, 0)

        def down(n, carry):
            cols = pl.ds(pl.multiple_of(n * 512, 512), 512)
            xs[yy, part, cols] = jnp.dot(
                hb[:count, :], wo[yy, :, cols], preferred_element_type=F32
            ).astype(BF16)
            return carry

        lax.fori_loop(0, D // 512, down, 0)

    def mlps(which, lo, hi):
        lax.fori_loop(which[0], which[1], lambda i, carry: (mlp(ring(y, i, NY), lo, hi), carry)[1], 0)

    dims = (((0,), (0,)), ((), ()))

    def weights(src):
        w = jnp.concatenate(
            [
                jnp.where(slot == mt[src, yy : yy + 1, :], mt[src, 4 + yy : 5 + yy, :], 0.0)
                for yy in range(NY)
            ],
            axis=0,
        )
        top = w.astype(BF16)
        return top, (w - top.astype(F32)).astype(BF16)

    def combined(pair, i, cols):
        rows = xs[:, i * CAP : (i + 1) * CAP, cols].reshape(NY * CAP, PIECE)
        got = lax.dot_general(pair[0], rows, dims, preferred_element_type=F32)
        return got + lax.dot_general(pair[1], rows, dims, preferred_element_type=F32)

    back = {}
    pieces = [pl.ds(j * PIECE, PIECE) for j in range(D // PIECE)]

    def send(way, k, j):
        i = k - 1 + (0 if way == "f" else 4)
        src = (zs_f if way == "f" else zs_b)[k]
        back[way, k - 1, j] = remote(
            tok.at[src, :, pieces[j]], rbuf.at[i, :, pieces[j]], to_z[1] if way == "f" else to_z[0]
        )

    def hop(way, k, i, js=range(D // PIECE)):
        src = (zs_f if way == "f" else zs_b)[k]
        last = k == (4 if way == "f" else 3)
        pair = weights(src)
        for j in js:
            if not last:
                if j == 0:
                    for t in t_z:
                        gone((t.f if way == "f" else t.b)[k + 1])
                back[way, k, j].wait_recv()
            got = combined(pair, i, pieces[j])
            if not last:
                got += rbuf[k + (0 if way == "f" else 4), :, pieces[j]].astype(F32)
            tok[src, :, pieces[j]] = got.astype(BF16)
            send(way, k, j)

    place(z, 0)
    i_x[0].step(1)
    t_z[0].step(1)
    i_x[1].step(1)
    i_x[2].start()
    local[5].wait()
    local[6].wait()
    local[7].wait()
    v_y.step(1)
    share(0, "y")
    share(1, "y")
    t_z[1].step(1)
    place(zs_f[1], 1)
    place(zs_b[1], 2)
    u_y.step(1)
    share(0, "o")
    share(1, "o")
    t_z[0].step(2)
    i_x[0].step_f(2)
    share(0, "x")
    i_x[1].step_f(2)
    share(1, "x")
    t_z[1].step(2)
    place(zs_f[2], 3)
    place(zs_b[2], 4)
    v_y.step_f(2)
    share(2, "y")
    i_x[2].step(1)
    mlp(y, 0, 5)
    t_z[0].step(3)
    have(0)
    mlp(others[0], 0, 5)
    u_y.step_f(2)
    share(2, "o")
    have(1)
    mlp(others[1], 0, 5)
    t_z[1].step(3)
    place(zs_f[3], 5)
    place(zs_b[3], 6)
    i_x[2].step_f(2)
    share(2, "x")
    mlps((NY - 1, NY + 2), 5, 7)
    have(2)
    mlp(others[2], 0, 7)
    hop("b", 3, 6)
    t_z[0].step_f(4)
    t_z[1].step_f(4)
    place(zs_f[4], 7)
    mlps((0, 2), 7, 8)
    hop("b", 2, 4, range(0, 2))
    mlps((2, 3), 7, 8)
    hop("b", 2, 4, range(2, 3))
    mlps((3, 4), 7, 8)
    hop("b", 2, 4, range(3, 4))
    hop("f", 4, 7)
    hop("b", 1, 2, range(0, 2))
    hop("f", 3, 5, range(0, 2))
    hop("b", 1, 2, range(2, 4))
    hop("f", 3, 5, range(2, 4))
    hop("f", 2, 3)
    hop("f", 1, 1)

    pair = weights(z)
    for j in range(D // PIECE):
        res[:, pieces[j]] = res[:, pieces[j]] + combined(pair, 0, pieces[j])
    for j in range(D // PIECE):
        back["b", 0, j].wait_recv()
        back["f", 0, j].wait_recv()
        both = rbuf[0, :, pieces[j]].astype(F32) + rbuf[4, :, pieces[j]].astype(F32)
        out[:, pieces[j]] = (res[:, pieces[j]] + both).astype(BF16)
    for copy in started:
        if id(copy) not in done:
            copy.wait_send()


def shards(resid, queries, span_kv, cache_kv, seg_len, o_rows, norm_gain, routes, route_wts, w_in, w_out):
    hbm = pl.BlockSpec(memory_space=pl.ANY)
    vmem = pl.BlockSpec(memory_space=pltpu.VMEM)
    dma = pltpu.SemaphoreType.DMA
    return pl.pallas_call(
        layer_kernel,
        out_shape=jax.ShapeDtypeStruct((SPAN, D), BF16),
        in_specs=[vmem] * 4 + [hbm] * 7,
        out_specs=vmem,
        scratch_shapes=[
            pltpu.VMEM((SPAN, D), BF16),
            pltpu.VMEM((2, 3, SPAN, D), BF16),
            pltpu.VMEM((8, SPAN), F32),
            pltpu.VMEM((8, SPAN), F32),
            pltpu.VMEM((NY, NZ, D // EXPERTS, HALF), BF16),
            pltpu.VMEM((2, SPAN, D), BF16),
            pltpu.VMEM((SPAN, HALF), F32),
            pltpu.VMEM((2, SPAN, HALF), F32),
            pltpu.VMEM((SPAN, D), F32),
            pltpu.VMEM((NZ, SPAN, D), BF16),
            pltpu.VMEM((NZ, 8, SPAN), F32),
            pltpu.VMEM((NZ, 8, SPAN), F32),
            pltpu.VMEM((NY, WY, 2 * FF), BF16),
            pltpu.VMEM((NY, D - WY, 2 * FF), BF16),
            pltpu.VMEM((NY, FF, D), BF16),
            pltpu.VMEM((NY, NZ * CAP, D), BF16),
            pltpu.VMEM((7 * CAP, FF), BF16),
            pltpu.VMEM((7, SPAN, D), BF16),
            dma((8,)),
            dma((160,)),
            dma((160,)),
        ],
        compiler_params=pltpu.CompilerParams(collective_id=0, has_side_effects=True, vmem_limit_bytes=62 << 20),
    )(
        routes.T,
        route_wts.T,
        seg_len,
        norm_gain.reshape(1, D),
        resid,
        queries,
        span_kv,
        cache_kv,
        o_rows,
        w_in,
        w_out,
    )


def solution(mesh):
    rows = P(("group", "expert"), None)
    placed = (
        rows,
        rows,
        P(None, ("group", "expert"), None),
        P(None, ("group", "expert"), None, None, None),
        rows,
        P("expert", None),
        P(),
        rows,
        rows,
        P("expert", None, None),
        P("expert", None, None),
    )
    return jax.shard_map(shards, mesh=mesh, in_specs=placed, out_specs=rows, check_vma=False)
```

```python
import functools
import math

import jax
import jax.numpy as jnp
from jax import lax
from jax.experimental import pallas as pl
from jax.experimental.pallas import tpu as pltpu
from jax.sharding import PartitionSpec as P

HEADS = 16
HD = 128
FF = 512
TOPK = 8
CAP = 48
NX, NY, NZ = 4, 4, 8
EXPERTS = NY * NZ
D = 2048
SPAN = 128
HALF = D // 2
OX = 128
OZ = HALF - NX * OX
WY = 640
PIECE = 512
MESH = pl.DeviceIdType.MESH
F32, BF16 = jnp.float32, jnp.bfloat16


def layer_kernel(
    routes, route_wts, seg_len, gain, resid, queries, span_kv, cache_kv, o_rows, w_in, w_out, out,
    qb, kv, segs, seg_out, obuf, att, pr, prs, res, tok, mine_t, mt, wiy, wix, wo, xs, hb, rbuf, loc, sent, came,
):
    g, e = lax.axis_index("group"), lax.axis_index("expert")
    x, c = g // 2, g % 2
    y, z = e // NZ, e % NZ
    f = 1 - 2 * c

    def ring(v, by, n):
        return lax.rem(v + by + 2 * n, n)

    def at(dx=0, dc=0, dy=0, dz=0):
        return (ring(x, dx, NX) * 2 + ring(c, dc, 2), ring(y, dy, NY) * NZ + ring(z, dz, NZ))

    sib = at(dc=1)
    x_peers = [at(dx=k) for k in (1, NX - 1)]
    y_peers = [at(dy=k) for k in (1, NY - 1, 2)]
    z_peers = [at(dz=k) for k in range(1, NZ)]
    peers = [sib] + x_peers + y_peers + z_peers
    barrier = pltpu.get_barrier_semaphore()
    for peer in peers:
        pl.semaphore_signal(barrier, inc=1, device_id=peer, device_id_type=MESH)

    half = c * HALF
    local = [
        pltpu.make_async_copy(o_rows.at[:, pl.ds(half, OZ)], obuf.at[0, z, :, pl.ds(0, OZ)], loc.at[0]),
        pltpu.make_async_copy(o_rows.at[:, pl.ds(half + OZ + x * OX, OX)], obuf.at[0, z, :, pl.ds(OZ, OX)], loc.at[1]),
        pltpu.make_async_copy(queries, qb, loc.at[2]),
        pltpu.make_async_copy(span_kv, kv.at[:, 0], loc.at[3]),
        pltpu.make_async_copy(cache_kv.at[:, 0, 0], kv.at[:, 1], loc.at[4]),
        pltpu.make_async_copy(w_in.at[:, pl.ds(0, WY)], wiy.at[pl.ds(y, 1)], loc.at[5]),
        pltpu.make_async_copy(w_in.at[:, pl.ds(WY, D - WY)], wix.at[pl.ds(y, 1)], loc.at[6]),
        pltpu.make_async_copy(w_out, wo.at[pl.ds(y, 1)], loc.at[7]),
    ]
    for copy in local[:5]:
        copy.start()
    seg_out[...] = jnp.broadcast_to(seg_len[:, 1:2].astype(F32), seg_out.shape)
    pl.semaphore_wait(barrier, len(peers))

    started, used, done = [], [0], set()

    def remote(src, dst, peer, slot=None):
        i = used[0] if slot is None else slot
        used[0] += slot is None
        copy = pltpu.make_async_remote_copy(
            src_ref=src, dst_ref=dst, send_sem=sent.at[i], recv_sem=came.at[i], device_id=peer, device_id_type=MESH
        )
        copy.start()
        started.append(copy)
        return copy

    def gone(copy):
        copy.wait_send()
        done.add(id(copy))

    def slots(n):
        i = used[0]
        used[0] += n
        return i

    def ring_slots(me, n):
        return [ring(me, -k * f, n) for k in range(n // 2 + 1)], [ring(me, k * f, n) for k in range(n // 2)]

    ys_f, ys_b = ring_slots(y, NY)
    zs_f, zs_b = ring_slots(z, NZ)
    xs_f, xs_b = ring_slots(x, NX)
    to_y, to_z, to_x = (at(dy=f), at(dy=-f)), (at(dz=f), at(dz=-f)), (at(dx=f), at(dx=-f))

    class Ring:
        def __init__(self, n, view, slots_f, slots_b, to, own=None, view_to=None):
            self.n, self.view, self.slots_f, self.slots_b, self.to = n, view, slots_f, slots_b, to
            self.own = view(slots_f[0]) if own is None else own
            self.view_to = view_to or (lambda s, way: view(s))
            self.base = slots(n - 1)
            self.f, self.b = {}, {}

        def put_f(self, k):
            src = self.own if k == 0 else self.view(self.slots_f[k])
            self.f[k + 1] = remote(src, self.view_to(self.slots_f[k], f), self.to[0], self.base + k)

        def put_b(self, k):
            src = self.own if k == 0 else self.view(self.slots_b[k])
            self.b[k + 1] = remote(src, self.view_to(self.slots_b[k], -f), self.to[1], self.base + self.n // 2 + k)

        def start(self):
            self.put_f(0)
            self.put_b(0)

        def step_f(self, k):
            self.f[k].wait_recv()
            if k < self.n // 2:
                self.put_f(k)

        def step_b(self, k):
            self.b[k].wait_recv()
            if k < self.n // 2 - 1:
                self.put_b(k)

        def step(self, k):
            self.step_f(k)
            if k < self.n // 2:
                self.step_b(k)

    zx = pl.ds(0, OZ + OX)
    local[0].wait()
    local[1].wait()
    o_y = [
        remote(obuf.at[0, z, :, zx], obuf.at[NY - k, z, :, zx], peer) for k, peer in zip((1, NY - 1, 2), y_peers)
    ]
    c_kv = remote(cache_kv.at[:, 0, 1], kv.at[:, 2], sib)
    c_seg = remote(seg_out, segs, sib)

    chunks = [pl.ds(OZ, OX)] + [pl.ds(k * (OZ // 2), OZ // 2) for k in range(2)]
    o_own = Ring(NZ, lambda s: obuf.at[0, s, :, zx], zs_f, zs_b, to_z)
    o_own.start()
    o_z = [
        Ring(NZ, functools.partial(lambda cols, s: obuf.at[pl.ds(1, NY - 1), s, :, cols], cols), zs_f, zs_b, to_z)
        for cols in chunks
    ]
    def shard_from(k, way):
        slots = [(-k * way_f) % NX if way == 0 else (-k * way_f - way * way_f) % NX for way_f in (1, -1)]
        return pl.ds(pl.multiple_of(OZ + (slots[0] + c * (slots[1] - slots[0])) * OX, OX), OX)

    class Spread:
        def __init__(self, zz):
            self.zz = zz
            self.f1 = self.send(0, 1)
            self.b1 = self.send(0, -1)

        def send(self, k, way):
            src, dst = obuf.at[:, self.zz, :, shard_from(k, 0)], obuf.at[:, self.zz, :, shard_from(k, way)]
            return remote(src, dst, to_x[0] if way == 1 else to_x[1])

        def step(self):
            self.f1.wait_recv()
            self.f2 = self.send(1, 1)

        def end(self):
            self.b1.wait_recv()
            self.f2.wait_recv()

    others = [ring(y, -1, NY), ring(y, 1, NY), ring(y, 2, NY)]
    deep = (D - WY) // 8

    def shard(s, start=0):
        return pl.ds(pl.multiple_of(start + (c * NX + s) * deep, 16), deep)

    def core_half(n):
        return pl.ds(pl.multiple_of(c * (n // 2), 16), n // 2)

    i_y = Ring(NY, lambda s: wix.at[s, shard(x)], ys_f, ys_b, to_y, own=w_in.at[0, shard(x, WY)])
    v_y = Ring(NY, lambda s: wiy.at[s, core_half(WY)], ys_f, ys_b, to_y, own=w_in.at[0, core_half(WY)])
    u_y = Ring(NY, lambda s: wo.at[s, core_half(FF)], ys_f, ys_b, to_y, own=w_out.at[0, core_half(FF)])
    i_x = [
        Ring(NX, functools.partial(lambda yy, s: wix.at[yy, shard(s)], yy), xs_f, xs_b, to_x)
        for yy in others
    ]
    w_sib, w_at = {}, slots(9)

    def share(i, what):
        yy = others[i]
        part = {"x": wix.at[yy, core_half(D - WY)], "y": wiy.at[yy, core_half(WY)], "o": wo.at[yy, core_half(FF)]}[what]
        w_sib[i, what] = remote(part, part, sib, w_at + 3 * i + "xyo".index(what))

    def have(i):
        for what in "yox":
            w_sib[i, what].wait_recv()

    lanes_e = lax.broadcasted_iota(jnp.int32, (EXPERTS, SPAN), 0).astype(F32)
    hit = jnp.zeros((EXPERTS, SPAN), F32)
    wts = jnp.zeros((EXPERTS, SPAN), F32)
    for k in range(TOPK):
        same = lanes_e == routes[k : k + 1, :].astype(F32)
        hit = jnp.where(same, 1.0, hit)
        wts = jnp.where(same, route_wts[k : k + 1, :], wts)
    rows_t = lax.broadcasted_iota(jnp.int32, (SPAN, SPAN), 0)
    cols_t = lax.broadcasted_iota(jnp.int32, (SPAN, SPAN), 1)
    earlier = (rows_t < cols_t).astype(F32).astype(BF16)
    before = jnp.dot(hit.astype(BF16), earlier, preferred_element_type=F32)
    pos = jnp.where(hit > 0.5, before, -1.0)
    for yy in range(NY):
        for zz in range(NZ):
            j = yy * NZ + zz
            mine_t[zz, yy : yy + 1, :] = pos[j : j + 1, :]
            mine_t[zz, 4 + yy : 5 + yy, :] = wts[j : j + 1, :]
    mt[z] = mine_t[z]
    metas = []
    for k in range(1, NZ):
        metas.append(remote(mine_t.at[ring(z, k, NZ)], mt.at[z], z_peers[k - 1]))

    for copy in local[2:5]:
        copy.wait()
    c_kv.wait_recv()
    c_seg.wait_recv()

    lane = lax.broadcasted_iota(jnp.int32, (1, SPAN), 1).astype(F32)
    valid = jnp.concatenate(
        [jnp.ones((1, SPAN), F32), (lane < seg_len[:, 0:1].astype(F32)).astype(F32), (lane < segs[0:1, :]).astype(F32)], axis=1
    )

    def head(h, carry):
        cols = pl.ds(pl.multiple_of(h * HD, HD), HD)
        q = qb[:, cols]
        keys = kv[0, :, :, cols].reshape(3 * SPAN, HD)
        vals = kv[1, :, :, cols].reshape(3 * SPAN, HD)
        s = lax.dot_general(q, keys, (((1,), (1,)), ((), ())), preferred_element_type=F32) * (1.0 / math.sqrt(HD))
        s = jnp.where(valid > 0.5, s, -1e30)
        m = jnp.max(s, axis=-1, keepdims=True)
        w = jnp.exp(s - m)
        total = jnp.sum(w, axis=-1, keepdims=True)
        a = jnp.dot(w.astype(BF16), vals, preferred_element_type=F32)
        att[c, :, cols] = (a / total).astype(BF16)
        return carry

    def heads(lo, hi):
        lax.fori_loop(lo, hi, head, 0)

    i_y.start()
    v_y.start()
    heads(0, 4)
    o_own.step(1)
    for copy in o_y:
        copy.wait_recv()
    o_z[0].start()
    s_own = Spread(z)
    for copy in local[5:]:
        copy.start()
    o_own.step(2)
    heads(4, 7)
    o_z[0].step(1)
    o_z[1].start()
    s_f1, s_b1 = Spread(zs_f[1]), Spread(zs_b[1])
    o_z[2].start()
    heads(7, 9)
    o_own.step(3)
    o_z[0].step(2)
    s_f2, s_b2 = Spread(zs_f[2]), Spread(zs_b[2])
    s_own.step()
    o_z[1].step(1)
    heads(9, 12)
    o_z[2].step(1)
    i_y.step(1)
    u_y.start()
    o_own.step(4)
    o_z[0].step(3)
    s_f3, s_b3 = Spread(zs_f[3]), Spread(zs_b[3])
    s_f1.step()
    s_b1.step()
    heads(12, 16)
    c_att = remote(att.at[c], att.at[c], sib)
    load = pltpu.make_async_copy(resid, qb, loc.at[2])
    load.start()
    o_z[1].step(2)
    o_z[0].step_f(4)
    s_f4 = Spread(zs_f[4])
    o_z[2].step(2)
    s_f2.step()
    s_b2.step()
    o_z[1].step(3)
    s_f3.step()
    s_b3.step()
    s_f4.step()
    o_z[2].step(3)
    i_x[0].start()
    for copy in metas:
        copy.wait_recv()
    c_att.wait_recv()
    o_z[1].step_f(4)
    o_z[2].step_f(4)
    for spread in (s_own, s_f1, s_b1, s_f2, s_b2, s_f3, s_b3, s_f4):
        spread.end()
    i_x[1].start()

    def columns(n):
        cols = pl.ds(pl.multiple_of(n * 256, 256), 256)
        total = jnp.zeros((2 * SPAN, 256), F32)
        for r in range(NY):
            depth = pl.ds(pl.multiple_of(ring(y, r, NY) * (D // NY), D // NY), D // NY)
            rows = att[:, :, depth].reshape(2 * SPAN, D // NY)
            total += jnp.dot(rows, obuf[r, :, :, cols].reshape(D // NY, 256), preferred_element_type=F32)
        return total.reshape(2, SPAN, 256)

    def project_z(n, carry):
        prs[:, :, pl.ds(pl.multiple_of(n * 256, 256), 256)] = columns(n)
        return carry

    def project_x(n):
        got = columns(OZ // 256 + n)
        for i in range(2):
            spot = pl.ds(pl.multiple_of(OZ + ring(x, 2 * n + i, NX) * OX, OX), OX)
            prs[:, :, spot] = got[:, :, i * OX : (i + 1) * OX]

    lax.fori_loop(0, OZ // 256, project_z, 0)
    for n in range(NX * OX // 256):
        project_x(n)
    c_pr = remote(prs.at[1 - c], pr, sib)
    load.wait()
    c_pr.wait_recv()
    mine = prs[c]
    theirs = pr[...]
    first = c == 0
    low = qb[:, :HALF].astype(F32) + jnp.where(first, mine, theirs)
    high = qb[:, HALF:].astype(F32) + jnp.where(first, theirs, mine)
    squares = jnp.sum(low * low, axis=-1, keepdims=True) + jnp.sum(high * high, axis=-1, keepdims=True)
    scale = lax.rsqrt(squares * (1.0 / D) + 1e-05)
    tok[z, :, :HALF] = (low * scale * gain[:, :HALF]).astype(BF16)
    t_z = [Ring(NZ, functools.partial(lambda j, s: tok.at[s, :, pl.ds(j * HALF, HALF)], j), zs_f, zs_b, to_z) for j in range(2)]
    t_z[0].start()
    tok[z, :, HALF:] = (high * scale * gain[:, HALF:]).astype(BF16)
    t_z[1].start()
    res[:, :HALF] = low
    res[:, HALF:] = high

    slot = lax.broadcasted_iota(jnp.int32, (CAP, SPAN), 0).astype(F32)

    def place(src, i):
        pick = jnp.concatenate(
            [jnp.where(slot == mt[src, yy : yy + 1, :], 1.0, 0.0) for yy in range(NY)], axis=0
        ).astype(BF16)

        def tile(n, carry):
            cols = pl.ds(pl.multiple_of(n * 512, 512), 512)
            rows = jnp.dot(pick, tok[src, :, cols], preferred_element_type=F32).astype(BF16)
            for yy in range(NY):
                xs[yy, i * CAP : (i + 1) * CAP, cols] = rows[yy * CAP : (yy + 1) * CAP]
            return carry

        lax.fori_loop(0, D // 512, tile, 0)

    def mlp(yy, lo, hi):
        part = slice(lo * CAP, hi * CAP)
        count = (hi - lo) * CAP

        def up(n, carry):
            gate = pl.ds(pl.multiple_of(n * 256, 256), 256)
            lift = pl.ds(pl.multiple_of(FF + n * 256, 256), 256)

            def times(cols):
                got = jnp.dot(xs[yy, part, :WY], wiy[yy, :, cols], preferred_element_type=F32)
                return got + jnp.dot(xs[yy, part, WY:], wix[yy, :, cols], preferred_element_type=F32)

            a, b = times(gate), times(lift)
            hb[:count, gate] = (a * (1.0 / (1.0 + jnp.exp(-a))) * b).astype(BF16)
            return carry

        lax.fori_loop(0, FF // 256, up, 0)

        def down(n, carry):
            cols = pl.ds(pl.multiple_of(n * 512, 512), 512)
            xs[yy, part, cols] = jnp.dot(
                hb[:count, :], wo[yy, :, cols], preferred_element_type=F32
            ).astype(BF16)
            return carry

        lax.fori_loop(0, D // 512, down, 0)

    def mlps(which, lo, hi):
        lax.fori_loop(which[0], which[1], lambda i, carry: (mlp(ring(y, i, NY), lo, hi), carry)[1], 0)

    dims = (((0,), (0,)), ((), ()))

    def weights(src):
        w = jnp.concatenate(
            [
                jnp.where(slot == mt[src, yy : yy + 1, :], mt[src, 4 + yy : 5 + yy, :], 0.0)
                for yy in range(NY)
            ],
            axis=0,
        )
        top = w.astype(BF16)
        return top, (w - top.astype(F32)).astype(BF16)

    def combined(pair, i, cols):
        rows = xs[:, i * CAP : (i + 1) * CAP, cols].reshape(NY * CAP, PIECE)
        got = lax.dot_general(pair[0], rows, dims, preferred_element_type=F32)
        return got + lax.dot_general(pair[1], rows, dims, preferred_element_type=F32)

    back = {}
    pieces = [pl.ds(j * PIECE, PIECE) for j in range(D // PIECE)]

    def send(way, k, j):
        i = k - 1 + (0 if way == "f" else 4)
        src = (zs_f if way == "f" else zs_b)[k]
        back[way, k - 1, j] = remote(
            tok.at[src, :, pieces[j]], rbuf.at[i, :, pieces[j]], to_z[1] if way == "f" else to_z[0]
        )

    def hop(way, k, i, js=range(D // PIECE)):
        src = (zs_f if way == "f" else zs_b)[k]
        last = k == (4 if way == "f" else 3)
        pair = weights(src)
        for j in js:
            if not last:
                if j == 0:
                    for t in t_z:
                        gone((t.f if way == "f" else t.b)[k + 1])
                back[way, k, j].wait_recv()
            got = combined(pair, i, pieces[j])
            if not last:
                got += rbuf[k + (0 if way == "f" else 4), :, pieces[j]].astype(F32)
            tok[src, :, pieces[j]] = got.astype(BF16)
            send(way, k, j)

    place(z, 0)
    i_x[0].step(1)
    t_z[0].step(1)
    i_y.step_f(2)
    i_x[1].step(1)
    i_x[2].start()
    local[5].wait()
    local[6].wait()
    local[7].wait()
    v_y.step(1)
    share(0, "y")
    share(1, "y")
    t_z[1].step(1)
    place(zs_f[1], 1)
    place(zs_b[1], 2)
    mlp(y, 0, 3)
    t_z[0].step(2)
    i_x[0].step_f(2)
    share(0, "x")
    u_y.step(1)
    share(0, "o")
    share(1, "o")
    t_z[1].step(2)
    i_x[1].step_f(2)
    share(1, "x")
    i_x[2].step(1)
    place(zs_f[2], 3)
    place(zs_b[2], 4)
    v_y.step_f(2)
    share(2, "y")
    have(0)
    mlp(others[0], 0, 5)
    t_z[0].step(3)
    have(1)
    mlp(others[1], 0, 5)
    i_x[2].step_f(2)
    share(2, "x")
    t_z[1].step(3)
    place(zs_b[3], 5)
    mlp(y, 3, 6)
    u_y.step_f(2)
    share(2, "o")
    mlp(others[0], 5, 6)
    mlp(others[1], 5, 6)
    have(2)
    mlp(others[2], 0, 6)
    hop("b", 3, 5)
    place(zs_f[3], 6)
    t_z[0].step_f(4)
    t_z[1].step_f(4)
    place(zs_f[4], 7)
    mlps((0, 2), 6, 8)
    hop("b", 2, 4, range(0, 2))
    mlps((2, 3), 6, 8)
    hop("b", 2, 4, range(2, 3))
    mlps((3, 4), 6, 8)
    hop("b", 2, 4, range(3, 4))
    hop("f", 4, 7)
    hop("b", 1, 2, range(0, 2))
    hop("f", 3, 6, range(0, 2))
    hop("b", 1, 2, range(2, 4))
    hop("f", 3, 6, range(2, 4))
    hop("f", 2, 3)
    hop("f", 1, 1)

    pair = weights(z)
    for j in range(D // PIECE):
        res[:, pieces[j]] = res[:, pieces[j]] + combined(pair, 0, pieces[j])
    for j in range(D // PIECE):
        back["b", 0, j].wait_recv()
        back["f", 0, j].wait_recv()
        both = rbuf[0, :, pieces[j]].astype(F32) + rbuf[4, :, pieces[j]].astype(F32)
        out[:, pieces[j]] = (res[:, pieces[j]] + both).astype(BF16)
    for copy in started:
        if id(copy) not in done:
            copy.wait_send()


def shards(resid, queries, span_kv, cache_kv, seg_len, o_rows, norm_gain, routes, route_wts, w_in, w_out):
    hbm = pl.BlockSpec(memory_space=pl.ANY)
    vmem = pl.BlockSpec(memory_space=pltpu.VMEM)
    dma = pltpu.SemaphoreType.DMA
    return pl.pallas_call(
        layer_kernel,
        out_shape=jax.ShapeDtypeStruct((SPAN, D), BF16),
        in_specs=[vmem] * 4 + [hbm] * 7,
        out_specs=vmem,
        scratch_shapes=[
            pltpu.VMEM((SPAN, D), BF16),
            pltpu.VMEM((2, 3, SPAN, D), BF16),
            pltpu.VMEM((8, SPAN), F32),
            pltpu.VMEM((8, SPAN), F32),
            pltpu.VMEM((NY, NZ, D // EXPERTS, HALF), BF16),
            pltpu.VMEM((2, SPAN, D), BF16),
            pltpu.VMEM((SPAN, HALF), F32),
            pltpu.VMEM((2, SPAN, HALF), F32),
            pltpu.VMEM((SPAN, D), F32),
            pltpu.VMEM((NZ, SPAN, D), BF16),
            pltpu.VMEM((NZ, 8, SPAN), F32),
            pltpu.VMEM((NZ, 8, SPAN), F32),
            pltpu.VMEM((NY, WY, 2 * FF), BF16),
            pltpu.VMEM((NY, D - WY, 2 * FF), BF16),
            pltpu.VMEM((NY, FF, D), BF16),
            pltpu.VMEM((NY, NZ * CAP, D), BF16),
            pltpu.VMEM((6 * CAP, FF), BF16),
            pltpu.VMEM((7, SPAN, D), BF16),
            dma((8,)),
            dma((160,)),
            dma((160,)),
        ],
        compiler_params=pltpu.CompilerParams(collective_id=0, has_side_effects=True, vmem_limit_bytes=62 << 20),
    )(
        routes.T,
        route_wts.T,
        seg_len,
        norm_gain.reshape(1, D),
        resid,
        queries,
        span_kv,
        cache_kv,
        o_rows,
        w_in,
        w_out,
    )


def solution(mesh):
    rows = P(("group", "expert"), None)
    placed = (
        rows,
        rows,
        P(None, ("group", "expert"), None),
        P(None, ("group", "expert"), None, None, None),
        rows,
        P("expert", None),
        P(),
        rows,
        rows,
        P("expert", None, None),
        P("expert", None, None),
    )
    return jax.shard_map(shards, mesh=mesh, in_specs=placed, out_specs=rows, check_vma=False)
```

```python
import functools
import math

import jax
import jax.numpy as jnp
from jax import lax
from jax.experimental import pallas as pl
from jax.experimental.pallas import tpu as pltpu
from jax.sharding import PartitionSpec as P

HEADS = 16
HD = 128
FF = 512
TOPK = 8
CAP = 48
NX, NY, NZ = 4, 4, 8
EXPERTS = NY * NZ
D = 2048
SPAN = 128
HALF = D // 2
OX = 128
OZ = HALF - NX * OX
WY = 640
PIECE = 512
MESH = pl.DeviceIdType.MESH
F32, BF16 = jnp.float32, jnp.bfloat16


def layer_kernel(
    routes, route_wts, seg_len, gain, resid, queries, span_kv, cache_kv, o_rows, w_in, w_out, out,
    qb, kv, segs, seg_out, obuf, att, pr, prs, res, tok, mine_t, mt, wiy, wix, wo, xs, hb, rbuf, loc, sent, came,
):
    g, e = lax.axis_index("group"), lax.axis_index("expert")
    x, c = g // 2, g % 2
    y, z = e // NZ, e % NZ
    f = 1 - 2 * c

    def ring(v, by, n):
        return lax.rem(v + by + 2 * n, n)

    def at(dx=0, dc=0, dy=0, dz=0):
        return (ring(x, dx, NX) * 2 + ring(c, dc, 2), ring(y, dy, NY) * NZ + ring(z, dz, NZ))

    sib = at(dc=1)
    x_peers = [at(dx=k) for k in (1, NX - 1)]
    y_peers = [at(dy=k) for k in (1, NY - 1, 2)]
    z_peers = [at(dz=k) for k in range(1, NZ)]
    peers = [sib] + x_peers + y_peers + z_peers
    barrier = pltpu.get_barrier_semaphore()
    for peer in peers:
        pl.semaphore_signal(barrier, inc=1, device_id=peer, device_id_type=MESH)

    half = c * HALF
    local = [
        pltpu.make_async_copy(o_rows.at[:, pl.ds(half, OZ)], obuf.at[0, z, :, pl.ds(0, OZ)], loc.at[0]),
        pltpu.make_async_copy(o_rows.at[:, pl.ds(half + OZ + x * OX, OX)], obuf.at[0, z, :, pl.ds(OZ, OX)], loc.at[1]),
        pltpu.make_async_copy(queries, qb, loc.at[2]),
        pltpu.make_async_copy(span_kv, kv.at[:, 0], loc.at[3]),
        pltpu.make_async_copy(cache_kv.at[:, 0, 0], kv.at[:, 1], loc.at[4]),
        pltpu.make_async_copy(w_in.at[:, pl.ds(0, WY)], wiy.at[pl.ds(y, 1)], loc.at[5]),
        pltpu.make_async_copy(w_in.at[:, pl.ds(WY, D - WY)], wix.at[pl.ds(y, 1)], loc.at[6]),
        pltpu.make_async_copy(w_out, wo.at[pl.ds(y, 1)], loc.at[7]),
    ]
    for copy in local[:5]:
        copy.start()
    seg_out[...] = jnp.broadcast_to(seg_len[:, 1:2].astype(F32), seg_out.shape)
    pl.semaphore_wait(barrier, len(peers))

    started, used, done = [], [0], set()

    def remote(src, dst, peer, slot=None):
        i = used[0] if slot is None else slot
        used[0] += slot is None
        copy = pltpu.make_async_remote_copy(
            src_ref=src, dst_ref=dst, send_sem=sent.at[i], recv_sem=came.at[i], device_id=peer, device_id_type=MESH
        )
        copy.start()
        started.append(copy)
        return copy

    def gone(copy):
        copy.wait_send()
        done.add(id(copy))

    def slots(n):
        i = used[0]
        used[0] += n
        return i

    def ring_slots(me, n):
        return [ring(me, -k * f, n) for k in range(n // 2 + 1)], [ring(me, k * f, n) for k in range(n // 2)]

    ys_f, ys_b = ring_slots(y, NY)
    zs_f, zs_b = ring_slots(z, NZ)
    xs_f, xs_b = ring_slots(x, NX)
    to_y, to_z, to_x = (at(dy=f), at(dy=-f)), (at(dz=f), at(dz=-f)), (at(dx=f), at(dx=-f))

    class Ring:
        def __init__(self, n, view, slots_f, slots_b, to, own=None, view_to=None):
            self.n, self.view, self.slots_f, self.slots_b, self.to = n, view, slots_f, slots_b, to
            self.own = view(slots_f[0]) if own is None else own
            self.view_to = view_to or (lambda s, way: view(s))
            self.base = slots(n - 1)
            self.f, self.b = {}, {}

        def put_f(self, k):
            src = self.own if k == 0 else self.view(self.slots_f[k])
            self.f[k + 1] = remote(src, self.view_to(self.slots_f[k], f), self.to[0], self.base + k)

        def put_b(self, k):
            src = self.own if k == 0 else self.view(self.slots_b[k])
            self.b[k + 1] = remote(src, self.view_to(self.slots_b[k], -f), self.to[1], self.base + self.n // 2 + k)

        def start(self):
            self.put_f(0)
            self.put_b(0)

        def step_f(self, k):
            self.f[k].wait_recv()
            if k < self.n // 2:
                self.put_f(k)

        def step_b(self, k):
            self.b[k].wait_recv()
            if k < self.n // 2 - 1:
                self.put_b(k)

        def step(self, k):
            self.step_f(k)
            if k < self.n // 2:
                self.step_b(k)

    zx = pl.ds(0, OZ + OX)
    local[0].wait()
    local[1].wait()
    o_y = [
        remote(obuf.at[0, z, :, zx], obuf.at[NY - k, z, :, zx], peer) for k, peer in zip((1, NY - 1, 2), y_peers)
    ]
    c_kv = remote(cache_kv.at[:, 0, 1], kv.at[:, 2], sib)
    c_seg = remote(seg_out, segs, sib)

    chunks = [pl.ds(OZ, OX)] + [pl.ds(k * (OZ // 2), OZ // 2) for k in range(2)]
    o_own = Ring(NZ, lambda s: obuf.at[0, s, :, zx], zs_f, zs_b, to_z)
    o_own.start()
    o_z = [
        Ring(NZ, functools.partial(lambda cols, s: obuf.at[pl.ds(1, NY - 1), s, :, cols], cols), zs_f, zs_b, to_z)
        for cols in chunks
    ]
    def shard_from(k, way):
        slots = [(-k * way_f) % NX if way == 0 else (-k * way_f - way * way_f) % NX for way_f in (1, -1)]
        return pl.ds(pl.multiple_of(OZ + (slots[0] + c * (slots[1] - slots[0])) * OX, OX), OX)

    class Spread:
        def __init__(self, zz):
            self.zz = zz
            self.f1 = self.send(0, 1)
            self.b1 = self.send(0, -1)

        def send(self, k, way):
            src, dst = obuf.at[:, self.zz, :, shard_from(k, 0)], obuf.at[:, self.zz, :, shard_from(k, way)]
            return remote(src, dst, to_x[0] if way == 1 else to_x[1])

        def step(self):
            self.f1.wait_recv()
            self.f2 = self.send(1, 1)

        def end(self):
            self.b1.wait_recv()
            self.f2.wait_recv()

    others = [ring(y, -1, NY), ring(y, 1, NY), ring(y, 2, NY)]
    deep = (D - WY) // 8

    def shard(s, start=0):
        return pl.ds(pl.multiple_of(start + (c * NX + s) * deep, 16), deep)

    def core_half(n):
        return pl.ds(pl.multiple_of(c * (n // 2), 16), n // 2)

    i_y = Ring(NY, lambda s: wix.at[s, shard(x)], ys_f, ys_b, to_y, own=w_in.at[0, shard(x, WY)])
    v_y = Ring(NY, lambda s: wiy.at[s, core_half(WY)], ys_f, ys_b, to_y, own=w_in.at[0, core_half(WY)])
    u_y = Ring(NY, lambda s: wo.at[s, core_half(FF)], ys_f, ys_b, to_y, own=w_out.at[0, core_half(FF)])
    i_x = [
        Ring(NX, functools.partial(lambda yy, s: wix.at[yy, shard(s)], yy), xs_f, xs_b, to_x)
        for yy in others
    ]
    w_sib, w_at = {}, slots(9)

    def share(i, what):
        yy = others[i]
        part = {"x": wix.at[yy, core_half(D - WY)], "y": wiy.at[yy, core_half(WY)], "o": wo.at[yy, core_half(FF)]}[what]
        w_sib[i, what] = remote(part, part, sib, w_at + 3 * i + "xyo".index(what))

    def have(i):
        for what in "yox":
            w_sib[i, what].wait_recv()

    lanes_e = lax.broadcasted_iota(jnp.int32, (EXPERTS, SPAN), 0).astype(F32)
    hit = jnp.zeros((EXPERTS, SPAN), F32)
    wts = jnp.zeros((EXPERTS, SPAN), F32)
    for k in range(TOPK):
        same = lanes_e == routes[k : k + 1, :].astype(F32)
        hit = jnp.where(same, 1.0, hit)
        wts = jnp.where(same, route_wts[k : k + 1, :], wts)
    rows_t = lax.broadcasted_iota(jnp.int32, (SPAN, SPAN), 0)
    cols_t = lax.broadcasted_iota(jnp.int32, (SPAN, SPAN), 1)
    earlier = (rows_t < cols_t).astype(F32).astype(BF16)
    before = jnp.dot(hit.astype(BF16), earlier, preferred_element_type=F32)
    pos = jnp.where(hit > 0.5, before, -1.0)
    for yy in range(NY):
        for zz in range(NZ):
            j = yy * NZ + zz
            mine_t[zz, yy : yy + 1, :] = pos[j : j + 1, :]
            mine_t[zz, 4 + yy : 5 + yy, :] = wts[j : j + 1, :]
    mt[z] = mine_t[z]
    metas = []
    for k in range(1, NZ):
        metas.append(remote(mine_t.at[ring(z, k, NZ)], mt.at[z], z_peers[k - 1]))

    for copy in local[2:5]:
        copy.wait()
    c_kv.wait_recv()
    c_seg.wait_recv()

    lane = lax.broadcasted_iota(jnp.int32, (1, SPAN), 1).astype(F32)
    valid = jnp.concatenate(
        [jnp.ones((1, SPAN), F32), (lane < seg_len[:, 0:1].astype(F32)).astype(F32), (lane < segs[0:1, :]).astype(F32)], axis=1
    )

    def head(h, carry):
        cols = pl.ds(pl.multiple_of(h * HD, HD), HD)
        q = qb[:, cols]
        keys = kv[0, :, :, cols].reshape(3 * SPAN, HD)
        vals = kv[1, :, :, cols].reshape(3 * SPAN, HD)
        s = lax.dot_general(q, keys, (((1,), (1,)), ((), ())), preferred_element_type=F32) * (1.0 / math.sqrt(HD))
        s = jnp.where(valid > 0.5, s, -1e30)
        m = jnp.max(s, axis=-1, keepdims=True)
        w = jnp.exp(s - m)
        total = jnp.sum(w, axis=-1, keepdims=True)
        a = jnp.dot(w.astype(BF16), vals, preferred_element_type=F32)
        att[c, :, cols] = (a / total).astype(BF16)
        return carry

    def heads(lo, hi):
        lax.fori_loop(lo, hi, head, 0)

    i_y.start()
    v_y.start()
    heads(0, 4)
    o_own.step(1)
    for copy in o_y:
        copy.wait_recv()
    o_z[0].start()
    s_own = Spread(z)
    for copy in local[5:]:
        copy.start()
    o_own.step(2)
    heads(4, 7)
    o_z[0].step(1)
    o_z[1].start()
    s_f1, s_b1 = Spread(zs_f[1]), Spread(zs_b[1])
    o_z[2].start()
    heads(7, 9)
    o_own.step(3)
    o_z[0].step(2)
    s_f2, s_b2 = Spread(zs_f[2]), Spread(zs_b[2])
    s_own.step()
    o_z[1].step(1)
    heads(9, 12)
    o_z[2].step(1)
    i_y.step(1)
    u_y.start()
    o_own.step(4)
    o_z[0].step(3)
    s_f3, s_b3 = Spread(zs_f[3]), Spread(zs_b[3])
    s_f1.step()
    s_b1.step()
    heads(12, 16)
    c_att = remote(att.at[c], att.at[c], sib)
    load = pltpu.make_async_copy(resid, qb, loc.at[2])
    load.start()
    o_z[1].step(2)
    o_z[0].step_f(4)
    s_f4 = Spread(zs_f[4])
    o_z[2].step(2)
    s_f2.step()
    s_b2.step()
    o_z[1].step(3)
    s_f3.step()
    s_b3.step()
    s_f4.step()
    o_z[2].step(3)
    i_x[0].start()
    for copy in metas:
        copy.wait_recv()
    c_att.wait_recv()
    o_z[1].step_f(4)
    o_z[2].step_f(4)
    for spread in (s_own, s_f1, s_b1, s_f2, s_b2, s_f3, s_b3, s_f4):
        spread.end()
    i_x[1].start()

    def columns(n):
        cols = pl.ds(pl.multiple_of(n * 256, 256), 256)
        total = jnp.zeros((2 * SPAN, 256), F32)
        for r in range(NY):
            depth = pl.ds(pl.multiple_of(ring(y, r, NY) * (D // NY), D // NY), D // NY)
            rows = att[:, :, depth].reshape(2 * SPAN, D // NY)
            total += jnp.dot(rows, obuf[r, :, :, cols].reshape(D // NY, 256), preferred_element_type=F32)
        return total.reshape(2, SPAN, 256)

    def project_z(n, carry):
        prs[:, :, pl.ds(pl.multiple_of(n * 256, 256), 256)] = columns(n)
        return carry

    def project_x(n):
        got = columns(OZ // 256 + n)
        for i in range(2):
            spot = pl.ds(pl.multiple_of(OZ + ring(x, 2 * n + i, NX) * OX, OX), OX)
            prs[:, :, spot] = got[:, :, i * OX : (i + 1) * OX]

    lax.fori_loop(0, OZ // 256, project_z, 0, unroll=True)
    for n in range(NX * OX // 256):
        project_x(n)
    c_pr = remote(prs.at[1 - c], pr, sib)
    load.wait()
    c_pr.wait_recv()
    mine = prs[c]
    theirs = pr[...]
    first = c == 0
    low = qb[:, :HALF].astype(F32) + jnp.where(first, mine, theirs)
    high = qb[:, HALF:].astype(F32) + jnp.where(first, theirs, mine)
    squares = jnp.sum(low * low, axis=-1, keepdims=True) + jnp.sum(high * high, axis=-1, keepdims=True)
    scale = lax.rsqrt(squares * (1.0 / D) + 1e-05)
    tok[z, :, :HALF] = (low * scale * gain[:, :HALF]).astype(BF16)
    t_z = [Ring(NZ, functools.partial(lambda j, s: tok.at[s, :, pl.ds(j * HALF, HALF)], j), zs_f, zs_b, to_z) for j in range(2)]
    t_z[0].start()
    tok[z, :, HALF:] = (high * scale * gain[:, HALF:]).astype(BF16)
    t_z[1].start()
    res[:, :HALF] = low
    res[:, HALF:] = high

    slot = lax.broadcasted_iota(jnp.int32, (CAP, SPAN), 0).astype(F32)

    def place(src, i):
        pick = jnp.concatenate(
            [jnp.where(slot == mt[src, yy : yy + 1, :], 1.0, 0.0) for yy in range(NY)], axis=0
        ).astype(BF16)

        def tile(n, carry):
            cols = pl.ds(pl.multiple_of(n * 512, 512), 512)
            rows = jnp.dot(pick, tok[src, :, cols], preferred_element_type=F32).astype(BF16)
            for yy in range(NY):
                xs[yy, i * CAP : (i + 1) * CAP, cols] = rows[yy * CAP : (yy + 1) * CAP]
            return carry

        lax.fori_loop(0, D // 512, tile, 0, unroll=True)

    def mlp(yy, lo, hi):
        part = slice(lo * CAP, hi * CAP)
        count = (hi - lo) * CAP

        def up(n, carry):
            gate = pl.ds(pl.multiple_of(n * 256, 256), 256)
            lift = pl.ds(pl.multiple_of(FF + n * 256, 256), 256)

            def times(cols):
                got = jnp.dot(xs[yy, part, :WY], wiy[yy, :, cols], preferred_element_type=F32)
                return got + jnp.dot(xs[yy, part, WY:], wix[yy, :, cols], preferred_element_type=F32)

            a, b = times(gate), times(lift)
            hb[:count, gate] = (a * (1.0 / (1.0 + jnp.exp(-a))) * b).astype(BF16)
            return carry

        lax.fori_loop(0, FF // 256, up, 0, unroll=count <= 3 * CAP)

        def down(n, carry):
            cols = pl.ds(pl.multiple_of(n * 512, 512), 512)
            xs[yy, part, cols] = jnp.dot(
                hb[:count, :], wo[yy, :, cols], preferred_element_type=F32
            ).astype(BF16)
            return carry

        lax.fori_loop(0, D // 512, down, 0, unroll=True)

    def mlps(which, lo, hi):
        lax.fori_loop(which[0], which[1], lambda i, carry: (mlp(ring(y, i, NY), lo, hi), carry)[1], 0)

    dims = (((0,), (0,)), ((), ()))

    def weights(src):
        w = jnp.concatenate(
            [
                jnp.where(slot == mt[src, yy : yy + 1, :], mt[src, 4 + yy : 5 + yy, :], 0.0)
                for yy in range(NY)
            ],
            axis=0,
        )
        top = w.astype(BF16)
        return top, (w - top.astype(F32)).astype(BF16)

    def combined(pair, i, cols):
        rows = xs[:, i * CAP : (i + 1) * CAP, cols].reshape(NY * CAP, PIECE)
        got = lax.dot_general(pair[0], rows, dims, preferred_element_type=F32)
        return got + lax.dot_general(pair[1], rows, dims, preferred_element_type=F32)

    back = {}
    pieces = [pl.ds(j * PIECE, PIECE) for j in range(D // PIECE)]

    def send(way, k, j):
        i = k - 1 + (0 if way == "f" else 4)
        src = (zs_f if way == "f" else zs_b)[k]
        back[way, k - 1, j] = remote(
            tok.at[src, :, pieces[j]], rbuf.at[i, :, pieces[j]], to_z[1] if way == "f" else to_z[0]
        )

    def hop(way, k, i, js=range(D // PIECE)):
        src = (zs_f if way == "f" else zs_b)[k]
        last = k == (4 if way == "f" else 3)
        pair = weights(src)
        for j in js:
            if not last:
                if j == 0:
                    for t in t_z:
                        gone((t.f if way == "f" else t.b)[k + 1])
                back[way, k, j].wait_recv()
            got = combined(pair, i, pieces[j])
            if not last:
                got += rbuf[k + (0 if way == "f" else 4), :, pieces[j]].astype(F32)
            tok[src, :, pieces[j]] = got.astype(BF16)
            send(way, k, j)

    v_y.step(1)
    share(0, "y")
    share(1, "y")
    place(z, 0)
    i_x[0].step(1)
    t_z[0].step(1)
    i_y.step_f(2)
    i_x[1].step(1)
    i_x[2].start()
    local[5].wait()
    local[6].wait()
    local[7].wait()
    t_z[1].step(1)
    place(zs_f[1], 1)
    u_y.step(1)
    share(0, "o")
    share(1, "o")
    place(zs_b[1], 2)
    mlp(y, 0, 3)
    t_z[0].step(2)
    i_x[0].step_f(2)
    share(0, "x")
    t_z[1].step(2)
    i_x[1].step_f(2)
    share(1, "x")
    i_x[2].step(1)
    place(zs_f[2], 3)
    place(zs_b[2], 4)
    v_y.step_f(2)
    share(2, "y")
    have(0)
    mlp(others[0], 0, 5)
    t_z[0].step(3)
    have(1)
    mlp(others[1], 0, 5)
    i_x[2].step_f(2)
    share(2, "x")
    t_z[1].step(3)
    place(zs_b[3], 5)
    mlp(y, 3, 6)
    u_y.step_f(2)
    share(2, "o")
    mlp(others[0], 5, 6)
    mlp(others[1], 5, 6)
    have(2)
    mlp(others[2], 0, 6)
    hop("b", 3, 5)
    place(zs_f[3], 6)
    t_z[0].step_f(4)
    t_z[1].step_f(4)
    place(zs_f[4], 7)
    mlps((0, 2), 6, 8)
    hop("b", 2, 4, range(0, 2))
    mlps((2, 3), 6, 8)
    hop("b", 2, 4, range(2, 3))
    mlps((3, 4), 6, 8)
    hop("b", 2, 4, range(3, 4))
    hop("f", 4, 7)
    hop("b", 1, 2, range(0, 2))
    hop("f", 3, 6, range(0, 2))
    hop("b", 1, 2, range(2, 4))
    hop("f", 3, 6, range(2, 4))
    hop("f", 2, 3)
    hop("f", 1, 1)

    pair = weights(z)
    for j in range(D // PIECE):
        res[:, pieces[j]] = res[:, pieces[j]] + combined(pair, 0, pieces[j])
    for j in range(D // PIECE):
        back["b", 0, j].wait_recv()
        back["f", 0, j].wait_recv()
        both = rbuf[0, :, pieces[j]].astype(F32) + rbuf[4, :, pieces[j]].astype(F32)
        out[:, pieces[j]] = (res[:, pieces[j]] + both).astype(BF16)
    for copy in started:
        if id(copy) not in done:
            copy.wait_send()


def shards(resid, queries, span_kv, cache_kv, seg_len, o_rows, norm_gain, routes, route_wts, w_in, w_out):
    hbm = pl.BlockSpec(memory_space=pl.ANY)
    vmem = pl.BlockSpec(memory_space=pltpu.VMEM)
    dma = pltpu.SemaphoreType.DMA
    return pl.pallas_call(
        layer_kernel,
        out_shape=jax.ShapeDtypeStruct((SPAN, D), BF16),
        in_specs=[vmem] * 4 + [hbm] * 7,
        out_specs=vmem,
        scratch_shapes=[
            pltpu.VMEM((SPAN, D), BF16),
            pltpu.VMEM((2, 3, SPAN, D), BF16),
            pltpu.VMEM((8, SPAN), F32),
            pltpu.VMEM((8, SPAN), F32),
            pltpu.VMEM((NY, NZ, D // EXPERTS, HALF), BF16),
            pltpu.VMEM((2, SPAN, D), BF16),
            pltpu.VMEM((SPAN, HALF), F32),
            pltpu.VMEM((2, SPAN, HALF), F32),
            pltpu.VMEM((SPAN, D), F32),
            pltpu.VMEM((NZ, SPAN, D), BF16),
            pltpu.VMEM((NZ, 8, SPAN), F32),
            pltpu.VMEM((NZ, 8, SPAN), F32),
            pltpu.VMEM((NY, WY, 2 * FF), BF16),
            pltpu.VMEM((NY, D - WY, 2 * FF), BF16),
            pltpu.VMEM((NY, FF, D), BF16),
            pltpu.VMEM((NY, NZ * CAP, D), BF16),
            pltpu.VMEM((6 * CAP, FF), BF16),
            pltpu.VMEM((7, SPAN, D), BF16),
            dma((8,)),
            dma((160,)),
            dma((160,)),
        ],
        compiler_params=pltpu.CompilerParams(collective_id=0, has_side_effects=True, vmem_limit_bytes=62 << 20),
    )(
        routes.T,
        route_wts.T,
        seg_len,
        norm_gain.reshape(1, D),
        resid,
        queries,
        span_kv,
        cache_kv,
        o_rows,
        w_in,
        w_out,
    )


def solution(mesh):
    rows = P(("group", "expert"), None)
    placed = (
        rows,
        rows,
        P(None, ("group", "expert"), None),
        P(None, ("group", "expert"), None, None, None),
        rows,
        P("expert", None),
        P(),
        rows,
        rows,
        P("expert", None, None),
        P("expert", None, None),
    )
    return jax.shard_map(shards, mesh=mesh, in_specs=placed, out_specs=rows, check_vma=False)
```

```python
import functools
import math

import jax
import jax.numpy as jnp
from jax import lax
from jax.experimental import pallas as pl
from jax.experimental.pallas import tpu as pltpu
from jax.sharding import PartitionSpec as P

HEADS = 16
HD = 128
FF = 512
TOPK = 8
CAP = 48
NX, NY, NZ = 4, 4, 8
EXPERTS = NY * NZ
D = 2048
SPAN = 128
HALF = D // 2
OX = 128
OZ = HALF - NX * OX
WY = 640
PIECE = 512
MESH = pl.DeviceIdType.MESH
F32, BF16 = jnp.float32, jnp.bfloat16


def layer_kernel(
    routes, route_wts, seg_len, gain, resid, queries, span_kv, cache_kv, o_rows, w_in, w_out, out,
    qb, kv, segs, seg_out, obuf, att, pr, prs, res, tok, mine_t, mt, wiy, wix, wo, xs, hb, rbuf, loc, sent, came,
):
    g, e = lax.axis_index("group"), lax.axis_index("expert")
    x, c = g // 2, g % 2
    y, z = e // NZ, e % NZ
    f = 1 - 2 * c

    def ring(v, by, n):
        return lax.rem(v + by + 2 * n, n)

    def at(dx=0, dc=0, dy=0, dz=0):
        return (ring(x, dx, NX) * 2 + ring(c, dc, 2), ring(y, dy, NY) * NZ + ring(z, dz, NZ))

    sib = at(dc=1)
    x_peers = [at(dx=k) for k in (1, NX - 1)]
    y_peers = [at(dy=k) for k in (1, NY - 1, 2)]
    z_peers = [at(dz=k) for k in range(1, NZ)]
    peers = [sib] + x_peers + y_peers + z_peers
    barrier = pltpu.get_barrier_semaphore()
    for peer in peers:
        pl.semaphore_signal(barrier, inc=1, device_id=peer, device_id_type=MESH)

    half = c * HALF
    local = [
        pltpu.make_async_copy(o_rows.at[:, pl.ds(half, OZ)], obuf.at[0, z, :, pl.ds(0, OZ)], loc.at[0]),
        pltpu.make_async_copy(o_rows.at[:, pl.ds(half + OZ + x * OX, OX)], obuf.at[0, z, :, pl.ds(OZ, OX)], loc.at[1]),
        pltpu.make_async_copy(queries, qb, loc.at[2]),
        pltpu.make_async_copy(span_kv, kv.at[:, 0], loc.at[3]),
        pltpu.make_async_copy(cache_kv.at[:, 0, 0], kv.at[:, 1], loc.at[4]),
        pltpu.make_async_copy(w_in.at[:, pl.ds(0, WY)], wiy.at[pl.ds(y, 1)], loc.at[5]),
        pltpu.make_async_copy(w_in.at[:, pl.ds(WY, D - WY)], wix.at[pl.ds(y, 1)], loc.at[6]),
        pltpu.make_async_copy(w_out, wo.at[pl.ds(y, 1)], loc.at[7]),
    ]
    for copy in local[:5]:
        copy.start()
    seg_out[...] = jnp.broadcast_to(seg_len[:, 1:2].astype(F32), seg_out.shape)
    pl.semaphore_wait(barrier, len(peers))

    started, used, done = [], [0], set()

    def remote(src, dst, peer, slot=None):
        i = used[0] if slot is None else slot
        used[0] += slot is None
        copy = pltpu.make_async_remote_copy(
            src_ref=src, dst_ref=dst, send_sem=sent.at[i], recv_sem=came.at[i], device_id=peer, device_id_type=MESH
        )
        copy.start()
        started.append(copy)
        return copy

    def gone(copy):
        copy.wait_send()
        done.add(id(copy))

    def slots(n):
        i = used[0]
        used[0] += n
        return i

    def ring_slots(me, n):
        return [ring(me, -k * f, n) for k in range(n // 2 + 1)], [ring(me, k * f, n) for k in range(n // 2)]

    ys_f, ys_b = ring_slots(y, NY)
    zs_f, zs_b = ring_slots(z, NZ)
    xs_f, xs_b = ring_slots(x, NX)
    to_y, to_z, to_x = (at(dy=f), at(dy=-f)), (at(dz=f), at(dz=-f)), (at(dx=f), at(dx=-f))

    class Ring:
        def __init__(self, n, view, slots_f, slots_b, to, own=None, view_to=None):
            self.n, self.view, self.slots_f, self.slots_b, self.to = n, view, slots_f, slots_b, to
            self.own = view(slots_f[0]) if own is None else own
            self.view_to = view_to or (lambda s, way: view(s))
            self.base = slots(n - 1)
            self.f, self.b = {}, {}

        def put_f(self, k):
            src = self.own if k == 0 else self.view(self.slots_f[k])
            self.f[k + 1] = remote(src, self.view_to(self.slots_f[k], f), self.to[0], self.base + k)

        def put_b(self, k):
            src = self.own if k == 0 else self.view(self.slots_b[k])
            self.b[k + 1] = remote(src, self.view_to(self.slots_b[k], -f), self.to[1], self.base + self.n // 2 + k)

        def start(self):
            self.put_f(0)
            self.put_b(0)

        def step_f(self, k):
            self.f[k].wait_recv()
            if k < self.n // 2:
                self.put_f(k)

        def step_b(self, k):
            self.b[k].wait_recv()
            if k < self.n // 2 - 1:
                self.put_b(k)

        def step(self, k):
            self.step_f(k)
            if k < self.n // 2:
                self.step_b(k)

    zx = pl.ds(0, OZ + OX)
    local[0].wait()
    local[1].wait()
    o_y = [
        remote(obuf.at[0, z, :, zx], obuf.at[NY - k, z, :, zx], peer) for k, peer in zip((1, NY - 1, 2), y_peers)
    ]
    c_kv = remote(cache_kv.at[:, 0, 1], kv.at[:, 2], sib)
    c_seg = remote(seg_out, segs, sib)

    chunks = [pl.ds(OZ, OX)] + [pl.ds(k * (OZ // 2), OZ // 2) for k in range(2)]
    o_own = Ring(NZ, lambda s: obuf.at[0, s, :, zx], zs_f, zs_b, to_z)
    o_own.start()
    o_z = [
        Ring(NZ, functools.partial(lambda cols, s: obuf.at[pl.ds(1, NY - 1), s, :, cols], cols), zs_f, zs_b, to_z)
        for cols in chunks
    ]
    def shard_from(k, way):
        slots = [(-k * way_f) % NX if way == 0 else (-k * way_f - way * way_f) % NX for way_f in (1, -1)]
        return pl.ds(pl.multiple_of(OZ + (slots[0] + c * (slots[1] - slots[0])) * OX, OX), OX)

    class Spread:
        def __init__(self, zz):
            self.zz = zz
            self.f1 = self.send(0, 1)
            self.b1 = self.send(0, -1)

        def send(self, k, way):
            src, dst = obuf.at[:, self.zz, :, shard_from(k, 0)], obuf.at[:, self.zz, :, shard_from(k, way)]
            return remote(src, dst, to_x[0] if way == 1 else to_x[1])

        def step(self):
            self.f1.wait_recv()
            self.f2 = self.send(1, 1)

        def end(self):
            self.b1.wait_recv()
            self.f2.wait_recv()

    others = [ring(y, -1, NY), ring(y, 1, NY), ring(y, 2, NY)]
    deep = (D - WY) // 8

    def shard(s, start=0):
        return pl.ds(pl.multiple_of(start + (c * NX + s) * deep, 16), deep)

    def core_half(n):
        return pl.ds(pl.multiple_of(c * (n // 2), 16), n // 2)

    i_y = Ring(NY, lambda s: wix.at[s, shard(x)], ys_f, ys_b, to_y, own=w_in.at[0, shard(x, WY)])
    v_y = Ring(NY, lambda s: wiy.at[s, core_half(WY)], ys_f, ys_b, to_y, own=w_in.at[0, core_half(WY)])
    u_y = Ring(NY, lambda s: wo.at[s, core_half(FF)], ys_f, ys_b, to_y, own=w_out.at[0, core_half(FF)])
    i_x = [
        Ring(NX, functools.partial(lambda yy, s: wix.at[yy, shard(s)], yy), xs_f, xs_b, to_x)
        for yy in others
    ]
    w_sib, w_at = {}, slots(9)

    def share(i, what):
        yy = others[i]
        part = {"x": wix.at[yy, core_half(D - WY)], "y": wiy.at[yy, core_half(WY)], "o": wo.at[yy, core_half(FF)]}[what]
        w_sib[i, what] = remote(part, part, sib, w_at + 3 * i + "xyo".index(what))

    def have(i):
        for what in "yox":
            w_sib[i, what].wait_recv()

    lanes_e = lax.broadcasted_iota(jnp.int32, (EXPERTS, SPAN), 0).astype(F32)
    hit = jnp.zeros((EXPERTS, SPAN), F32)
    wts = jnp.zeros((EXPERTS, SPAN), F32)
    for k in range(TOPK):
        same = lanes_e == routes[k : k + 1, :].astype(F32)
        hit = jnp.where(same, 1.0, hit)
        wts = jnp.where(same, route_wts[k : k + 1, :], wts)
    rows_t = lax.broadcasted_iota(jnp.int32, (SPAN, SPAN), 0)
    cols_t = lax.broadcasted_iota(jnp.int32, (SPAN, SPAN), 1)
    earlier = (rows_t < cols_t).astype(F32).astype(BF16)
    before = jnp.dot(hit.astype(BF16), earlier, preferred_element_type=F32)
    pos = jnp.where(hit > 0.5, before, -1.0)
    for yy in range(NY):
        for zz in range(NZ):
            j = yy * NZ + zz
            mine_t[zz, yy : yy + 1, :] = pos[j : j + 1, :]
            mine_t[zz, 4 + yy : 5 + yy, :] = wts[j : j + 1, :]
    mt[z] = mine_t[z]
    metas = []
    for k in range(1, NZ):
        metas.append(remote(mine_t.at[ring(z, k, NZ)], mt.at[z], z_peers[k - 1]))

    for copy in local[2:5]:
        copy.wait()
    c_kv.wait_recv()
    c_seg.wait_recv()

    lane = lax.broadcasted_iota(jnp.int32, (1, SPAN), 1).astype(F32)
    valid = jnp.concatenate(
        [jnp.ones((1, SPAN), F32), (lane < seg_len[:, 0:1].astype(F32)).astype(F32), (lane < segs[0:1, :]).astype(F32)], axis=1
    )

    def head(h, carry):
        cols = pl.ds(pl.multiple_of(h * HD, HD), HD)
        q = qb[:, cols]
        keys = kv[0, :, :, cols].reshape(3 * SPAN, HD)
        vals = kv[1, :, :, cols].reshape(3 * SPAN, HD)
        s = lax.dot_general(q, keys, (((1,), (1,)), ((), ())), preferred_element_type=F32) * (1.0 / math.sqrt(HD))
        s = jnp.where(valid > 0.5, s, -1e30)
        m = jnp.max(s, axis=-1, keepdims=True)
        w = jnp.exp(s - m)
        total = jnp.sum(w, axis=-1, keepdims=True)
        a = jnp.dot(w.astype(BF16), vals, preferred_element_type=F32)
        att[c, :, cols] = (a / total).astype(BF16)
        return carry

    def heads(lo, hi):
        lax.fori_loop(lo, hi, head, 0)

    i_y.start()
    v_y.start()
    heads(0, 4)
    o_own.step(1)
    for copy in o_y:
        copy.wait_recv()
    o_z[0].start()
    s_own = Spread(z)
    for copy in local[5:]:
        copy.start()
    o_own.step(2)
    heads(4, 7)
    o_z[0].step(1)
    o_z[1].start()
    s_f1, s_b1 = Spread(zs_f[1]), Spread(zs_b[1])
    o_z[2].start()
    heads(7, 9)
    o_own.step(3)
    o_z[0].step(2)
    s_f2, s_b2 = Spread(zs_f[2]), Spread(zs_b[2])
    s_own.step()
    o_z[1].step(1)
    heads(9, 12)
    o_z[2].step(1)
    i_y.step(1)
    u_y.start()
    o_own.step(4)
    o_z[0].step(3)
    s_f3, s_b3 = Spread(zs_f[3]), Spread(zs_b[3])
    s_f1.step()
    s_b1.step()
    heads(12, 16)
    c_att = remote(att.at[c], att.at[c], sib)
    load = pltpu.make_async_copy(resid, qb, loc.at[2])
    load.start()
    o_z[1].step(2)
    o_z[0].step_f(4)
    s_f4 = Spread(zs_f[4])
    o_z[2].step(2)
    s_f2.step()
    s_b2.step()
    o_z[1].step(3)
    s_f3.step()
    s_b3.step()
    s_f4.step()
    o_z[2].step(3)
    i_x[0].start()
    for copy in metas:
        copy.wait_recv()
    c_att.wait_recv()
    o_z[1].step_f(4)
    o_z[2].step_f(4)
    for spread in (s_own, s_f1, s_b1, s_f2, s_b2, s_f3, s_b3, s_f4):
        spread.end()
    i_x[1].start()

    def columns(n):
        cols = pl.ds(pl.multiple_of(n * 256, 256), 256)
        total = jnp.zeros((2 * SPAN, 256), F32)
        for r in range(NY):
            depth = pl.ds(pl.multiple_of(ring(y, r, NY) * (D // NY), D // NY), D // NY)
            rows = att[:, :, depth].reshape(2 * SPAN, D // NY)
            total += jnp.dot(rows, obuf[r, :, :, cols].reshape(D // NY, 256), preferred_element_type=F32)
        return total.reshape(2, SPAN, 256)

    def project_z(n, carry):
        prs[:, :, pl.ds(pl.multiple_of(n * 256, 256), 256)] = columns(n)
        return carry

    def project_x(n):
        got = columns(OZ // 256 + n)
        for i in range(2):
            spot = pl.ds(pl.multiple_of(OZ + ring(x, 2 * n + i, NX) * OX, OX), OX)
            prs[:, :, spot] = got[:, :, i * OX : (i + 1) * OX]

    lax.fori_loop(0, OZ // 256, project_z, 0, unroll=True)
    for n in range(NX * OX // 256):
        project_x(n)
    c_pr = remote(prs.at[1 - c], pr, sib)
    load.wait()
    c_pr.wait_recv()
    mine = prs[c]
    theirs = pr[...]
    first = c == 0
    low = qb[:, :HALF].astype(F32) + jnp.where(first, mine, theirs)
    high = qb[:, HALF:].astype(F32) + jnp.where(first, theirs, mine)
    squares = jnp.sum(low * low, axis=-1, keepdims=True) + jnp.sum(high * high, axis=-1, keepdims=True)
    scale = lax.rsqrt(squares * (1.0 / D) + 1e-05)
    tok[z, :, :HALF] = (low * scale * gain[:, :HALF]).astype(BF16)
    t_z = [Ring(NZ, functools.partial(lambda j, s: tok.at[s, :, pl.ds(j * HALF, HALF)], j), zs_f, zs_b, to_z) for j in range(2)]
    t_z[0].start()
    tok[z, :, HALF:] = (high * scale * gain[:, HALF:]).astype(BF16)
    t_z[1].start()
    res[:, :HALF] = low
    res[:, HALF:] = high

    slot = lax.broadcasted_iota(jnp.int32, (CAP, SPAN), 0).astype(F32)

    def place(src, i):
        pick = jnp.concatenate(
            [jnp.where(slot == mt[src, yy : yy + 1, :], 1.0, 0.0) for yy in range(NY)], axis=0
        ).astype(BF16)

        def tile(n, carry):
            cols = pl.ds(pl.multiple_of(n * 512, 512), 512)
            rows = jnp.dot(pick, tok[src, :, cols], preferred_element_type=F32).astype(BF16)
            for yy in range(NY):
                xs[yy, i * CAP : (i + 1) * CAP, cols] = rows[yy * CAP : (yy + 1) * CAP]
            return carry

        lax.fori_loop(0, D // 512, tile, 0, unroll=True)

    def mlp(yy, lo, hi):
        part = slice(lo * CAP, hi * CAP)
        count = (hi - lo) * CAP

        def up(n, carry):
            gate = pl.ds(pl.multiple_of(n * 256, 256), 256)
            lift = pl.ds(pl.multiple_of(FF + n * 256, 256), 256)

            def times(cols):
                got = jnp.dot(xs[yy, part, :WY], wiy[yy, :, cols], preferred_element_type=F32)
                return got + jnp.dot(xs[yy, part, WY:], wix[yy, :, cols], preferred_element_type=F32)

            a, b = times(gate), times(lift)
            hb[:count, gate] = (a * (1.0 / (1.0 + jnp.exp(-a))) * b).astype(BF16)
            return carry

        lax.fori_loop(0, FF // 256, up, 0, unroll=True)

        def down(n, carry):
            cols = pl.ds(pl.multiple_of(n * 512, 512), 512)
            xs[yy, part, cols] = jnp.dot(
                hb[:count, :], wo[yy, :, cols], preferred_element_type=F32
            ).astype(BF16)
            return carry

        lax.fori_loop(0, D // 512, down, 0, unroll=True)

    def mlps(which, lo, hi):
        lax.fori_loop(which[0], which[1], lambda i, carry: (mlp(ring(y, i, NY), lo, hi), carry)[1], 0, unroll=True)

    dims = (((0,), (0,)), ((), ()))

    def weights(src):
        w = jnp.concatenate(
            [
                jnp.where(slot == mt[src, yy : yy + 1, :], mt[src, 4 + yy : 5 + yy, :], 0.0)
                for yy in range(NY)
            ],
            axis=0,
        )
        top = w.astype(BF16)
        return top, (w - top.astype(F32)).astype(BF16)

    def combined(pair, i, cols):
        rows = xs[:, i * CAP : (i + 1) * CAP, cols].reshape(NY * CAP, PIECE)
        got = lax.dot_general(pair[0], rows, dims, preferred_element_type=F32)
        return got + lax.dot_general(pair[1], rows, dims, preferred_element_type=F32)

    back = {}
    pieces = [pl.ds(j * PIECE, PIECE) for j in range(D // PIECE)]

    def send(way, k, j):
        i = k - 1 + (0 if way == "f" else 4)
        src = (zs_f if way == "f" else zs_b)[k]
        back[way, k - 1, j] = remote(
            tok.at[src, :, pieces[j]], rbuf.at[i, :, pieces[j]], to_z[1] if way == "f" else to_z[0]
        )

    def hop(way, k, i, js=range(D // PIECE)):
        src = (zs_f if way == "f" else zs_b)[k]
        last = k == (4 if way == "f" else 3)
        pair = weights(src)
        for j in js:
            if not last:
                if j == 0:
                    for t in t_z:
                        gone((t.f if way == "f" else t.b)[k + 1])
                back[way, k, j].wait_recv()
            got = combined(pair, i, pieces[j])
            if not last:
                got += rbuf[k + (0 if way == "f" else 4), :, pieces[j]].astype(F32)
            tok[src, :, pieces[j]] = got.astype(BF16)
            send(way, k, j)

    v_y.step(1)
    share(0, "y")
    share(1, "y")
    place(z, 0)
    i_x[0].step(1)
    t_z[0].step(1)
    i_y.step_f(2)
    i_x[1].step(1)
    i_x[2].start()
    local[5].wait()
    local[6].wait()
    local[7].wait()
    t_z[1].step(1)
    place(zs_f[1], 1)
    u_y.step(1)
    share(0, "o")
    share(1, "o")
    place(zs_b[1], 2)
    mlp(y, 0, 3)
    t_z[0].step(2)
    i_x[0].step_f(2)
    share(0, "x")
    t_z[1].step(2)
    i_x[1].step_f(2)
    share(1, "x")
    i_x[2].step(1)
    place(zs_f[2], 3)
    place(zs_b[2], 4)
    v_y.step_f(2)
    share(2, "y")
    have(0)
    mlp(others[0], 0, 5)
    t_z[0].step(3)
    have(1)
    mlp(others[1], 0, 5)
    i_x[2].step_f(2)
    share(2, "x")
    t_z[1].step(3)
    place(zs_b[3], 5)
    u_y.step_f(2)
    share(2, "o")
    mlp(y, 3, 6)
    mlp(others[0], 5, 6)
    mlp(others[1], 5, 6)
    have(2)
    mlp(others[2], 0, 6)
    hop("b", 3, 5)
    place(zs_f[3], 6)
    t_z[0].step_f(4)
    t_z[1].step_f(4)
    place(zs_f[4], 7)
    mlps((0, 2), 6, 8)
    hop("b", 2, 4, range(0, 2))
    mlps((2, 3), 6, 8)
    hop("b", 2, 4, range(2, 3))
    mlps((3, 4), 6, 8)
    hop("b", 2, 4, range(3, 4))
    hop("f", 4, 7)
    hop("b", 1, 2, range(0, 2))
    hop("f", 3, 6, range(0, 2))
    hop("b", 1, 2, range(2, 4))
    hop("f", 3, 6, range(2, 4))
    hop("f", 2, 3)
    hop("f", 1, 1)

    pair = weights(z)
    for j in range(D // PIECE):
        res[:, pieces[j]] = res[:, pieces[j]] + combined(pair, 0, pieces[j])
    for j in range(D // PIECE):
        back["b", 0, j].wait_recv()
        back["f", 0, j].wait_recv()
        both = rbuf[0, :, pieces[j]].astype(F32) + rbuf[4, :, pieces[j]].astype(F32)
        out[:, pieces[j]] = (res[:, pieces[j]] + both).astype(BF16)
    for copy in started:
        if id(copy) not in done:
            copy.wait_send()


def shards(resid, queries, span_kv, cache_kv, seg_len, o_rows, norm_gain, routes, route_wts, w_in, w_out):
    hbm = pl.BlockSpec(memory_space=pl.ANY)
    vmem = pl.BlockSpec(memory_space=pltpu.VMEM)
    dma = pltpu.SemaphoreType.DMA
    return pl.pallas_call(
        layer_kernel,
        out_shape=jax.ShapeDtypeStruct((SPAN, D), BF16),
        in_specs=[vmem] * 4 + [hbm] * 7,
        out_specs=vmem,
        scratch_shapes=[
            pltpu.VMEM((SPAN, D), BF16),
            pltpu.VMEM((2, 3, SPAN, D), BF16),
            pltpu.VMEM((8, SPAN), F32),
            pltpu.VMEM((8, SPAN), F32),
            pltpu.VMEM((NY, NZ, D // EXPERTS, HALF), BF16),
            pltpu.VMEM((2, SPAN, D), BF16),
            pltpu.VMEM((SPAN, HALF), F32),
            pltpu.VMEM((2, SPAN, HALF), F32),
            pltpu.VMEM((SPAN, D), F32),
            pltpu.VMEM((NZ, SPAN, D), BF16),
            pltpu.VMEM((NZ, 8, SPAN), F32),
            pltpu.VMEM((NZ, 8, SPAN), F32),
            pltpu.VMEM((NY, WY, 2 * FF), BF16),
            pltpu.VMEM((NY, D - WY, 2 * FF), BF16),
            pltpu.VMEM((NY, FF, D), BF16),
            pltpu.VMEM((NY, NZ * CAP, D), BF16),
            pltpu.VMEM((6 * CAP, FF), BF16),
            pltpu.VMEM((7, SPAN, D), BF16),
            dma((8,)),
            dma((160,)),
            dma((160,)),
        ],
        compiler_params=pltpu.CompilerParams(collective_id=0, has_side_effects=True, vmem_limit_bytes=62 << 20),
    )(
        routes.T,
        route_wts.T,
        seg_len,
        norm_gain.reshape(1, D),
        resid,
        queries,
        span_kv,
        cache_kv,
        o_rows,
        w_in,
        w_out,
    )


def solution(mesh):
    rows = P(("group", "expert"), None)
    placed = (
        rows,
        rows,
        P(None, ("group", "expert"), None),
        P(None, ("group", "expert"), None, None, None),
        rows,
        P("expert", None),
        P(),
        rows,
        rows,
        P("expert", None, None),
        P("expert", None, None),
    )
    return jax.shard_map(shards, mesh=mesh, in_specs=placed, out_specs=rows, check_vma=False)
```

```python
import functools
import math

import jax
import jax.numpy as jnp
from jax import lax
from jax.experimental import pallas as pl
from jax.experimental.pallas import tpu as pltpu
from jax.sharding import PartitionSpec as P

HEADS = 16
HD = 128
FF = 512
TOPK = 8
CAP = 48
NX, NY, NZ = 4, 4, 8
EXPERTS = NY * NZ
D = 2048
SPAN = 128
HALF = D // 2
OX = 128
OZ = HALF - NX * OX
WY = 640
PIECE = 512
MESH = pl.DeviceIdType.MESH
F32, BF16 = jnp.float32, jnp.bfloat16


def layer_kernel(
    routes, route_wts, seg_len, gain, resid, queries, span_kv, cache_kv, o_rows, w_in, w_out, out,
    qb, kv, segs, seg_out, obuf, att, pr, prs, res, tok, mine_t, mt, wiy, wix, wo, xs, hb, rbuf, loc, sent, came,
):
    g, e = lax.axis_index("group"), lax.axis_index("expert")
    x, c = g // 2, g % 2
    y, z = e // NZ, e % NZ
    f = 1 - 2 * c

    def ring(v, by, n):
        return lax.rem(v + by + 2 * n, n)

    def at(dx=0, dc=0, dy=0, dz=0):
        return (ring(x, dx, NX) * 2 + ring(c, dc, 2), ring(y, dy, NY) * NZ + ring(z, dz, NZ))

    sib = at(dc=1)
    x_peers = [at(dx=k) for k in (1, NX - 1)]
    y_peers = [at(dy=k) for k in (1, NY - 1, 2)]
    z_peers = [at(dz=k) for k in range(1, NZ)]
    peers = [sib] + x_peers + y_peers + z_peers
    barrier = pltpu.get_barrier_semaphore()
    for peer in peers:
        pl.semaphore_signal(barrier, inc=1, device_id=peer, device_id_type=MESH)

    half = c * HALF
    local = [
        pltpu.make_async_copy(o_rows.at[:, pl.ds(half, OZ)], obuf.at[0, z, :, pl.ds(0, OZ)], loc.at[0]),
        pltpu.make_async_copy(o_rows.at[:, pl.ds(half + OZ + x * OX, OX)], obuf.at[0, z, :, pl.ds(OZ, OX)], loc.at[1]),
        pltpu.make_async_copy(queries, qb, loc.at[2]),
        pltpu.make_async_copy(span_kv, kv.at[:, 0], loc.at[3]),
        pltpu.make_async_copy(cache_kv.at[:, 0, 0], kv.at[:, 1], loc.at[4]),
        pltpu.make_async_copy(w_in.at[:, pl.ds(0, WY)], wiy.at[pl.ds(y, 1)], loc.at[5]),
        pltpu.make_async_copy(w_in.at[:, pl.ds(WY, D - WY)], wix.at[pl.ds(y, 1)], loc.at[6]),
        pltpu.make_async_copy(w_out, wo.at[pl.ds(y, 1)], loc.at[7]),
    ]
    for copy in local[:5]:
        copy.start()
    seg_out[...] = jnp.broadcast_to(seg_len[:, 1:2].astype(F32), seg_out.shape)
    pl.semaphore_wait(barrier, len(peers))

    started, used, done = [], [0], set()

    def remote(src, dst, peer, slot=None):
        i = used[0] if slot is None else slot
        used[0] += slot is None
        copy = pltpu.make_async_remote_copy(
            src_ref=src, dst_ref=dst, send_sem=sent.at[i], recv_sem=came.at[i], device_id=peer, device_id_type=MESH
        )
        copy.start()
        started.append(copy)
        return copy

    def gone(copy):
        copy.wait_send()
        done.add(id(copy))

    def slots(n):
        i = used[0]
        used[0] += n
        return i

    def ring_slots(me, n):
        return [ring(me, -k * f, n) for k in range(n // 2 + 1)], [ring(me, k * f, n) for k in range(n // 2)]

    ys_f, ys_b = ring_slots(y, NY)
    zs_f, zs_b = ring_slots(z, NZ)
    xs_f, xs_b = ring_slots(x, NX)
    to_y, to_z, to_x = (at(dy=f), at(dy=-f)), (at(dz=f), at(dz=-f)), (at(dx=f), at(dx=-f))

    class Ring:
        def __init__(self, n, view, slots_f, slots_b, to, own=None, view_to=None):
            self.n, self.view, self.slots_f, self.slots_b, self.to = n, view, slots_f, slots_b, to
            self.own = view(slots_f[0]) if own is None else own
            self.view_to = view_to or (lambda s, way: view(s))
            self.base = slots(n - 1)
            self.f, self.b = {}, {}

        def put_f(self, k):
            src = self.own if k == 0 else self.view(self.slots_f[k])
            self.f[k + 1] = remote(src, self.view_to(self.slots_f[k], f), self.to[0], self.base + k)

        def put_b(self, k):
            src = self.own if k == 0 else self.view(self.slots_b[k])
            self.b[k + 1] = remote(src, self.view_to(self.slots_b[k], -f), self.to[1], self.base + self.n // 2 + k)

        def start(self):
            self.put_f(0)
            self.put_b(0)

        def step_f(self, k):
            self.f[k].wait_recv()
            if k < self.n // 2:
                self.put_f(k)

        def step_b(self, k):
            self.b[k].wait_recv()
            if k < self.n // 2 - 1:
                self.put_b(k)

        def step(self, k):
            self.step_f(k)
            if k < self.n // 2:
                self.step_b(k)

    zx = pl.ds(0, OZ + OX)
    local[0].wait()
    local[1].wait()
    o_y = [
        remote(obuf.at[0, z, :, zx], obuf.at[NY - k, z, :, zx], peer) for k, peer in zip((1, NY - 1, 2), y_peers)
    ]
    c_kv = remote(cache_kv.at[:, 0, 1], kv.at[:, 2], sib)
    c_seg = remote(seg_out, segs, sib)

    chunks = [pl.ds(OZ, OX)] + [pl.ds(k * (OZ // 2), OZ // 2) for k in range(2)]
    o_own = Ring(NZ, lambda s: obuf.at[0, s, :, zx], zs_f, zs_b, to_z)
    o_own.start()
    o_z = [
        Ring(NZ, functools.partial(lambda cols, s: obuf.at[pl.ds(1, NY - 1), s, :, cols], cols), zs_f, zs_b, to_z)
        for cols in chunks
    ]
    def shard_from(k, way):
        slots = [(-k * way_f) % NX if way == 0 else (-k * way_f - way * way_f) % NX for way_f in (1, -1)]
        return pl.ds(pl.multiple_of(OZ + (slots[0] + c * (slots[1] - slots[0])) * OX, OX), OX)

    class Spread:
        def __init__(self, zz):
            self.zz = zz
            self.f1 = self.send(0, 1)
            self.b1 = self.send(0, -1)

        def send(self, k, way):
            src, dst = obuf.at[:, self.zz, :, shard_from(k, 0)], obuf.at[:, self.zz, :, shard_from(k, way)]
            return remote(src, dst, to_x[0] if way == 1 else to_x[1])

        def step(self):
            self.f1.wait_recv()
            self.f2 = self.send(1, 1)

        def end(self):
            self.b1.wait_recv()
            self.f2.wait_recv()

    others = [ring(y, -1, NY), ring(y, 1, NY), ring(y, 2, NY)]
    deep = (D - WY) // 8

    def shard(s, start=0):
        return pl.ds(pl.multiple_of(start + (c * NX + s) * deep, 16), deep)

    def core_half(n):
        return pl.ds(pl.multiple_of(c * (n // 2), 16), n // 2)

    i_y = Ring(NY, lambda s: wix.at[s, shard(x)], ys_f, ys_b, to_y, own=w_in.at[0, shard(x, WY)])
    v_y = Ring(NY, lambda s: wiy.at[s, core_half(WY)], ys_f, ys_b, to_y, own=w_in.at[0, core_half(WY)])
    u_y = Ring(NY, lambda s: wo.at[s, core_half(FF)], ys_f, ys_b, to_y, own=w_out.at[0, core_half(FF)])
    i_x = [
        Ring(NX, functools.partial(lambda yy, s: wix.at[yy, shard(s)], yy), xs_f, xs_b, to_x)
        for yy in others
    ]
    w_sib, w_at = {}, slots(9)

    def share(i, what):
        yy = others[i]
        part = {"x": wix.at[yy, core_half(D - WY)], "y": wiy.at[yy, core_half(WY)], "o": wo.at[yy, core_half(FF)]}[what]
        w_sib[i, what] = remote(part, part, sib, w_at + 3 * i + "xyo".index(what))

    def have(i):
        for what in "yox":
            w_sib[i, what].wait_recv()

    lanes_e = lax.broadcasted_iota(jnp.int32, (EXPERTS, SPAN), 0).astype(F32)
    hit = jnp.zeros((EXPERTS, SPAN), F32)
    wts = jnp.zeros((EXPERTS, SPAN), F32)
    for k in range(TOPK):
        same = lanes_e == routes[k : k + 1, :].astype(F32)
        hit = jnp.where(same, 1.0, hit)
        wts = jnp.where(same, route_wts[k : k + 1, :], wts)
    rows_t = lax.broadcasted_iota(jnp.int32, (SPAN, SPAN), 0)
    cols_t = lax.broadcasted_iota(jnp.int32, (SPAN, SPAN), 1)
    earlier = (rows_t < cols_t).astype(F32).astype(BF16)
    before = jnp.dot(hit.astype(BF16), earlier, preferred_element_type=F32)
    pos = jnp.where(hit > 0.5, before, -1.0)
    for yy in range(NY):
        for zz in range(NZ):
            j = yy * NZ + zz
            mine_t[zz, yy : yy + 1, :] = pos[j : j + 1, :]
            mine_t[zz, 4 + yy : 5 + yy, :] = wts[j : j + 1, :]
    mt[z] = mine_t[z]
    metas = []
    for k in range(1, NZ):
        metas.append(remote(mine_t.at[ring(z, k, NZ)], mt.at[z], z_peers[k - 1]))

    for copy in local[2:5]:
        copy.wait()
    c_kv.wait_recv()
    c_seg.wait_recv()

    lane = lax.broadcasted_iota(jnp.int32, (1, SPAN), 1).astype(F32)
    valid = jnp.concatenate(
        [jnp.ones((1, SPAN), F32), (lane < seg_len[:, 0:1].astype(F32)).astype(F32), (lane < segs[0:1, :]).astype(F32)], axis=1
    )

    def head(h, carry):
        cols = pl.ds(pl.multiple_of(h * HD, HD), HD)
        q = qb[:, cols]
        keys = kv[0, :, :, cols].reshape(3 * SPAN, HD)
        vals = kv[1, :, :, cols].reshape(3 * SPAN, HD)
        s = lax.dot_general(q, keys, (((1,), (1,)), ((), ())), preferred_element_type=F32) * (1.0 / math.sqrt(HD))
        s = jnp.where(valid > 0.5, s, -1e30)
        m = jnp.max(s, axis=-1, keepdims=True)
        w = jnp.exp(s - m)
        total = jnp.sum(w, axis=-1, keepdims=True)
        a = jnp.dot(w.astype(BF16), vals, preferred_element_type=F32)
        att[c, :, cols] = (a / total).astype(BF16)
        return carry

    def heads(lo, hi):
        lax.fori_loop(lo, hi, head, 0, unroll=True)

    i_y.start()
    v_y.start()
    heads(0, 4)
    o_own.step(1)
    for copy in o_y:
        copy.wait_recv()
    o_z[0].start()
    s_own = Spread(z)
    for copy in local[5:]:
        copy.start()
    o_own.step(2)
    heads(4, 7)
    o_z[0].step(1)
    o_z[1].start()
    s_f1, s_b1 = Spread(zs_f[1]), Spread(zs_b[1])
    o_z[2].start()
    heads(7, 9)
    o_own.step(3)
    o_z[0].step(2)
    s_f2, s_b2 = Spread(zs_f[2]), Spread(zs_b[2])
    s_own.step()
    o_z[1].step(1)
    heads(9, 12)
    o_z[2].step(1)
    i_y.step(1)
    u_y.start()
    o_own.step(4)
    o_z[0].step(3)
    s_f3, s_b3 = Spread(zs_f[3]), Spread(zs_b[3])
    s_f1.step()
    s_b1.step()
    heads(12, 16)
    c_att = remote(att.at[c], att.at[c], sib)
    load = pltpu.make_async_copy(resid, qb, loc.at[2])
    load.start()
    o_z[1].step(2)
    o_z[0].step_f(4)
    s_f4 = Spread(zs_f[4])
    o_z[2].step(2)
    s_f2.step()
    s_b2.step()
    o_z[1].step(3)
    s_f3.step()
    s_b3.step()
    s_f4.step()
    o_z[2].step(3)
    i_x[0].start()
    for copy in metas:
        copy.wait_recv()
    c_att.wait_recv()
    o_z[1].step_f(4)
    o_z[2].step_f(4)
    for spread in (s_own, s_f1, s_b1, s_f2, s_b2, s_f3, s_b3, s_f4):
        spread.end()
    i_x[1].start()

    def columns(n):
        cols = pl.ds(pl.multiple_of(n * 256, 256), 256)
        total = jnp.zeros((2 * SPAN, 256), F32)
        for r in range(NY):
            depth = pl.ds(pl.multiple_of(ring(y, r, NY) * (D // NY), D // NY), D // NY)
            rows = att[:, :, depth].reshape(2 * SPAN, D // NY)
            total += jnp.dot(rows, obuf[r, :, :, cols].reshape(D // NY, 256), preferred_element_type=F32)
        return total.reshape(2, SPAN, 256)

    def project_z(n, carry):
        prs[:, :, pl.ds(pl.multiple_of(n * 256, 256), 256)] = columns(n)
        return carry

    def project_x(n):
        got = columns(OZ // 256 + n)
        for i in range(2):
            spot = pl.ds(pl.multiple_of(OZ + ring(x, 2 * n + i, NX) * OX, OX), OX)
            prs[:, :, spot] = got[:, :, i * OX : (i + 1) * OX]

    lax.fori_loop(0, OZ // 256, project_z, 0, unroll=True)
    for n in range(NX * OX // 256):
        project_x(n)
    c_pr = remote(prs.at[1 - c], pr, sib)
    load.wait()
    c_pr.wait_recv()
    mine = prs[c]
    theirs = pr[...]
    first = c == 0
    low = qb[:, :HALF].astype(F32) + jnp.where(first, mine, theirs)
    high = qb[:, HALF:].astype(F32) + jnp.where(first, theirs, mine)
    squares = jnp.sum(low * low, axis=-1, keepdims=True) + jnp.sum(high * high, axis=-1, keepdims=True)
    scale = lax.rsqrt(squares * (1.0 / D) + 1e-05)
    tok[z, :, :HALF] = (low * scale * gain[:, :HALF]).astype(BF16)
    t_z = [Ring(NZ, functools.partial(lambda j, s: tok.at[s, :, pl.ds(j * HALF, HALF)], j), zs_f, zs_b, to_z) for j in range(2)]
    t_z[0].start()
    tok[z, :, HALF:] = (high * scale * gain[:, HALF:]).astype(BF16)
    t_z[1].start()
    res[:, :HALF] = low
    res[:, HALF:] = high

    slot = lax.broadcasted_iota(jnp.int32, (CAP, SPAN), 0).astype(F32)

    def place(src, i):
        pick = jnp.concatenate(
            [jnp.where(slot == mt[src, yy : yy + 1, :], 1.0, 0.0) for yy in range(NY)], axis=0
        ).astype(BF16)

        def tile(n, carry):
            cols = pl.ds(pl.multiple_of(n * 512, 512), 512)
            rows = jnp.dot(pick, tok[src, :, cols], preferred_element_type=F32).astype(BF16)
            for yy in range(NY):
                xs[yy, i * CAP : (i + 1) * CAP, cols] = rows[yy * CAP : (yy + 1) * CAP]
            return carry

        lax.fori_loop(0, D // 512, tile, 0, unroll=True)

    def mlp(yy, lo, hi):
        part = slice(lo * CAP, hi * CAP)
        count = (hi - lo) * CAP

        def up(n, carry):
            gate = pl.ds(pl.multiple_of(n * 256, 256), 256)
            lift = pl.ds(pl.multiple_of(FF + n * 256, 256), 256)

            def times(cols):
                got = jnp.dot(xs[yy, part, :WY], wiy[yy, :, cols], preferred_element_type=F32)
                return got + jnp.dot(xs[yy, part, WY:], wix[yy, :, cols], preferred_element_type=F32)

            a, b = times(gate), times(lift)
            hb[:count, gate] = (a * (1.0 / (1.0 + jnp.exp(-a))) * b).astype(BF16)
            return carry

        lax.fori_loop(0, FF // 256, up, 0, unroll=True)

        def down(n, carry):
            cols = pl.ds(pl.multiple_of(n * 512, 512), 512)
            xs[yy, part, cols] = jnp.dot(
                hb[:count, :], wo[yy, :, cols], preferred_element_type=F32
            ).astype(BF16)
            return carry

        lax.fori_loop(0, D // 512, down, 0, unroll=True)

    def mlps(which, lo, hi):
        lax.fori_loop(which[0], which[1], lambda i, carry: (mlp(ring(y, i, NY), lo, hi), carry)[1], 0, unroll=True)

    dims = (((0,), (0,)), ((), ()))

    def weights(src):
        w = jnp.concatenate(
            [
                jnp.where(slot == mt[src, yy : yy + 1, :], mt[src, 4 + yy : 5 + yy, :], 0.0)
                for yy in range(NY)
            ],
            axis=0,
        )
        top = w.astype(BF16)
        return top, (w - top.astype(F32)).astype(BF16)

    def combined(pair, i, cols):
        rows = xs[:, i * CAP : (i + 1) * CAP, cols].reshape(NY * CAP, PIECE)
        got = lax.dot_general(pair[0], rows, dims, preferred_element_type=F32)
        return got + lax.dot_general(pair[1], rows, dims, preferred_element_type=F32)

    back = {}
    pieces = [pl.ds(j * PIECE, PIECE) for j in range(D // PIECE)]

    def send(way, k, j):
        i = k - 1 + (0 if way == "f" else 4)
        src = (zs_f if way == "f" else zs_b)[k]
        back[way, k - 1, j] = remote(
            tok.at[src, :, pieces[j]], rbuf.at[i, :, pieces[j]], to_z[1] if way == "f" else to_z[0]
        )

    def hop(way, k, i, js=range(D // PIECE)):
        src = (zs_f if way == "f" else zs_b)[k]
        last = k == (4 if way == "f" else 3)
        pair = weights(src)
        for j in js:
            if not last:
                if j == 0:
                    for t in t_z:
                        gone((t.f if way == "f" else t.b)[k + 1])
                back[way, k, j].wait_recv()
            got = combined(pair, i, pieces[j])
            if not last:
                got += rbuf[k + (0 if way == "f" else 4), :, pieces[j]].astype(F32)
            tok[src, :, pieces[j]] = got.astype(BF16)
            send(way, k, j)

    v_y.step(1)
    share(0, "y")
    share(1, "y")
    place(z, 0)
    i_x[0].step(1)
    t_z[0].step(1)
    i_y.step_f(2)
    i_x[1].step(1)
    i_x[2].start()
    local[5].wait()
    local[6].wait()
    local[7].wait()
    t_z[1].step(1)
    place(zs_f[1], 1)
    u_y.step(1)
    share(0, "o")
    share(1, "o")
    place(zs_b[1], 2)
    mlp(y, 0, 3)
    t_z[0].step(2)
    i_x[0].step_f(2)
    share(0, "x")
    t_z[1].step(2)
    i_x[1].step_f(2)
    share(1, "x")
    i_x[2].step(1)
    place(zs_f[2], 3)
    place(zs_b[2], 4)
    v_y.step_f(2)
    share(2, "y")
    have(0)
    mlp(others[0], 0, 5)
    t_z[0].step(3)
    have(1)
    mlp(others[1], 0, 5)
    i_x[2].step_f(2)
    share(2, "x")
    t_z[1].step(3)
    place(zs_b[3], 5)
    u_y.step_f(2)
    share(2, "o")
    mlp(y, 3, 6)
    mlp(others[0], 5, 6)
    mlp(others[1], 5, 6)
    have(2)
    mlp(others[2], 0, 6)
    hop("b", 3, 5)
    place(zs_f[3], 6)
    t_z[0].step_f(4)
    t_z[1].step_f(4)
    place(zs_f[4], 7)
    mlps((0, 2), 6, 8)
    hop("b", 2, 4, range(0, 2))
    mlps((2, 3), 6, 8)
    hop("b", 2, 4, range(2, 3))
    mlps((3, 4), 6, 8)
    hop("b", 2, 4, range(3, 4))
    hop("f", 4, 7)
    hop("b", 1, 2, range(0, 2))
    hop("f", 3, 6, range(0, 2))
    hop("b", 1, 2, range(2, 4))
    hop("f", 3, 6, range(2, 4))
    hop("f", 2, 3)
    hop("f", 1, 1)

    pair = weights(z)
    for j in range(D // PIECE):
        res[:, pieces[j]] = res[:, pieces[j]] + combined(pair, 0, pieces[j])
    for j in range(D // PIECE):
        back["b", 0, j].wait_recv()
        back["f", 0, j].wait_recv()
        both = rbuf[0, :, pieces[j]].astype(F32) + rbuf[4, :, pieces[j]].astype(F32)
        out[:, pieces[j]] = (res[:, pieces[j]] + both).astype(BF16)
    for copy in started:
        if id(copy) not in done:
            copy.wait_send()


def shards(resid, queries, span_kv, cache_kv, seg_len, o_rows, norm_gain, routes, route_wts, w_in, w_out):
    hbm = pl.BlockSpec(memory_space=pl.ANY)
    vmem = pl.BlockSpec(memory_space=pltpu.VMEM)
    dma = pltpu.SemaphoreType.DMA
    return pl.pallas_call(
        layer_kernel,
        out_shape=jax.ShapeDtypeStruct((SPAN, D), BF16),
        in_specs=[vmem] * 4 + [hbm] * 7,
        out_specs=vmem,
        scratch_shapes=[
            pltpu.VMEM((SPAN, D), BF16),
            pltpu.VMEM((2, 3, SPAN, D), BF16),
            pltpu.VMEM((8, SPAN), F32),
            pltpu.VMEM((8, SPAN), F32),
            pltpu.VMEM((NY, NZ, D // EXPERTS, HALF), BF16),
            pltpu.VMEM((2, SPAN, D), BF16),
            pltpu.VMEM((SPAN, HALF), F32),
            pltpu.VMEM((2, SPAN, HALF), F32),
            pltpu.VMEM((SPAN, D), F32),
            pltpu.VMEM((NZ, SPAN, D), BF16),
            pltpu.VMEM((NZ, 8, SPAN), F32),
            pltpu.VMEM((NZ, 8, SPAN), F32),
            pltpu.VMEM((NY, WY, 2 * FF), BF16),
            pltpu.VMEM((NY, D - WY, 2 * FF), BF16),
            pltpu.VMEM((NY, FF, D), BF16),
            pltpu.VMEM((NY, NZ * CAP, D), BF16),
            pltpu.VMEM((6 * CAP, FF), BF16),
            pltpu.VMEM((7, SPAN, D), BF16),
            dma((8,)),
            dma((160,)),
            dma((160,)),
        ],
        compiler_params=pltpu.CompilerParams(collective_id=0, has_side_effects=True, vmem_limit_bytes=62 << 20),
    )(
        routes.T,
        route_wts.T,
        seg_len,
        norm_gain.reshape(1, D),
        resid,
        queries,
        span_kv,
        cache_kv,
        o_rows,
        w_in,
        w_out,
    )


def solution(mesh):
    rows = P(("group", "expert"), None)
    placed = (
        rows,
        rows,
        P(None, ("group", "expert"), None),
        P(None, ("group", "expert"), None, None, None),
        rows,
        P("expert", None),
        P(),
        rows,
        rows,
        P("expert", None, None),
        P("expert", None, None),
    )
    return jax.shard_map(shards, mesh=mesh, in_specs=placed, out_specs=rows, check_vma=False)
```
